256 devices in a mesh: strike: 16 (over x, y), depth: 16 (over z, core).
Axes of the slice: x: 4, y: 4, z: 8, core: 2. Of those that a mesh axis runs over, the one named last changes fastest.
Arguments:
- dof_values: float32 [9, 35, 32768], P(None, None, ('strike', 'depth')), may hold values from -6 to 6
- star_matrices: float32 [3, 9, 9, 32768], P(None, None, None, ('strike', 'depth')), may hold values from -2 to 2
- flux_solvers: float32 [2, 4, 9, 9, 32768], P(None, None, None, None, ('strike', 'depth')), may hold values from -1 to 1
- stiffness: float32 [3, 35, 35], replicated, may hold values from -1.5 to 1.5
- flux_local: float32 [4, 35, 35], replicated, may hold values from -1 to 1
- flux_neighbour: float32 [48, 35, 35], replicated, may hold values from -1 to 1
- flux_select: int32 [4, 32768], P(None, ('strike', 'depth')), may hold values from 0 to 47
- face_source: int32 [4, 32768], P(None, ('strike', 'depth')), may hold values from 0 to 639, as said below
- side_list: int32 [4, 32768], P(None, ('strike', 'depth')), may hold values from 0 to 127
- cluster_ids: int32 [32768], P(('strike', 'depth')), may hold values from 0 to 1, as said below
- damage: float32 [32768], P(('strike', 'depth')), may hold values from 0 to 0.5
- element_size: float32 [32768], P(('strike', 'depth')), may hold values from 1 to 9
- wave_speed: float32 [32768], P(('strike', 'depth')), may hold values from 1 to 2
- damage_rate: float32 [32768], P(('strike', 'depth')), may hold values from 0.5 to 4
Outputs:
- dof_next: float32 [9, 35, 32768], P(None, None, ('strike', 'depth'))
- damage_next: float32 [32768], P(('strike', 'depth'))
- next_step: float32 [], replicated
The draws below stay inside these ranges and needn't reach their ends.
Inputs may be any that keep to these rules, and one draw needn't show every extreme that they name: `face_source`: within each partition's block, entries below 128 name its own elements and the others the received slots, four blocks of 128 in the order strike-1, strike+1, depth-1, depth+1; every slot is named by some face. `cluster_ids`: within each partition's block the elements of cluster 0 come first; there are from 16 to 64 of them, 64 in some partition.
All inputs are finite; a program needn't handle non-finite values.
Results may differ from the reference program's by a relative error of at most 0.0003.
Values sent between devices are 32-bit elements; how exact they have to be, the bound alone decides.
A program may use at most 128 MiB of HBM per device.

```python
import math
import jax
import jax.numpy as jnp
import numpy as np
from jax import lax

Q = 9
B = 35
NSEL = 48
E_DEV = 128
SIDE = 128
FMAX = 64
ELEMS = 32768
SIDES = 32768
N_STRIKE = 16
N_DEPTH = 16


def draw_face_source(key, part):
    key = jax.random.fold_in(key, 11)
    count = ELEMS // E_DEV

    def one_block(index):
        sub_key = jax.random.fold_in(key, index)
        local_rows = jax.random.randint(jax.random.fold_in(sub_key, 1), (4 * E_DEV,), 0, E_DEV)
        shuffled = jax.random.permutation(jax.random.fold_in(sub_key, 2), 4 * E_DEV)
        local_rows = local_rows.at[shuffled[:4 * SIDE]].set(E_DEV + jnp.arange(4 * SIDE, dtype=jnp.int32))
        return local_rows.reshape(4, E_DEV)
    blocks = jax.vmap(one_block)(jnp.arange(count, dtype=jnp.int32))
    return jnp.moveaxis(blocks, 0, 1).reshape(4, ELEMS).astype(jnp.int32)


def draw_cluster_ids(key, part):
    key = jax.random.fold_in(key, 12)
    count = ELEMS // E_DEV
    filled = jax.random.randint(jax.random.fold_in(key, 1), (count,), FMAX // 4, FMAX + 1)
    fullest = jax.random.randint(jax.random.fold_in(key, 2), (), 0, count)
    filled = filled.at[fullest].set(FMAX)
    positions = jnp.arange(E_DEV, dtype=jnp.int32)
    return (positions[None, :] >= filled[:, None]).astype(jnp.int32).reshape(ELEMS)


def draw_element_size(key, part):
    key = jax.random.fold_in(key, 13)
    count = ELEMS // E_DEV
    blocks = (jnp.arange(ELEMS, dtype=jnp.int32) // E_DEV).astype(jnp.float32)
    position = blocks / max(count - 1, 1)
    rough = jnp.exp(jax.random.uniform(key, (ELEMS,), jnp.float32, 0.0, jnp.log(3.0)))
    return ((1.0 + 2.0 * position) * rough).astype(jnp.float32)


def set_ends(values, stream_key, low, top_value):
    shape = values.shape
    place = [jax.random.randint(jax.random.fold_in(stream_key, axis), (), 0, shape[axis]) for axis in range(len(shape))]
    values = values.at[tuple(place)].set(low)
    longest = shape.index(max(shape))
    place[longest] = (place[longest] + 1) % shape[longest]
    return values.at[tuple(place)].set(top_value)


def steps_of(stream_key, extent, shards, least, high):
    level, own = 1.0, jax.random.fold_in(stream_key, 6)
    for dim, blocks in shards:
        draws = jnp.exp(jax.random.uniform(jax.random.fold_in(own, dim), (blocks,), jnp.float32, least / len(shards), high / len(shards)))
        level = level * jnp.repeat(draws, extent[dim] // blocks).reshape([-1 if axis == dim else 1 for axis in range(len(extent))])
    return level


def centred(own_key, dims, scale, most, shards=(), kind=jnp.bfloat16):
    entries = scale * jax.random.normal(own_key, dims, jnp.float32)
    if shards:
        entries = entries * steps_of(own_key, dims, shards, -0.22, 0.18)
    return jnp.clip(entries, -most, most).astype(kind)


def setup_inputs(seed: int = 0) -> dict:
    streams_of = jax.random.split(jax.random.key(seed), 15)
    dof_values = centred(streams_of[0], (Q, B, ELEMS), 1.0, 6.0, ((2, 256),), jnp.float32)
    star_matrices = centred(streams_of[1], (3, Q, Q, ELEMS), Q ** -0.5, 2.0, ((3, 256),), jnp.float32)
    flux_solvers = centred(streams_of[2], (2, 4, Q, Q, ELEMS), (4 * Q) ** -0.5, 1.0, ((4, 256),), jnp.float32)
    stiffness = centred(streams_of[3], (3, B, B), (B // 2) ** -0.5, 1.5, (), jnp.float32)
    flux_local = centred(streams_of[4], (4, B, B), B ** -0.5, 1.0, (), jnp.float32)
    flux_neighbour = centred(streams_of[5], (NSEL, B, B), B ** -0.5, 1.0, (), jnp.float32)
    flux_select = set_ends(jax.random.randint(streams_of[6], (4, ELEMS), 0, NSEL), jax.random.fold_in(streams_of[6], 1), 0, NSEL - 1).astype(jnp.int32)
    face_source = draw_face_source(jax.random.fold_in(streams_of[14], 71), 0)
    side_list = set_ends(jax.random.randint(streams_of[8], (4, SIDES), 0, E_DEV), jax.random.fold_in(streams_of[8], 1), 0, E_DEV - 1).astype(jnp.int32)
    cluster_ids = draw_cluster_ids(jax.random.fold_in(streams_of[14], 71), 0)
    damage = jnp.clip(0.5 * jax.random.uniform(streams_of[10], (ELEMS,), jnp.float32) ** steps_of(streams_of[10], (ELEMS,), ((0, 256),), -0.2, 0.2), 0.0, 0.5)
    element_size = draw_element_size(jax.random.fold_in(streams_of[14], 71), 0)
    wave_speed = jnp.clip(1.0 + 1.0 * jax.random.uniform(streams_of[12], (ELEMS,), jnp.float32) ** steps_of(streams_of[12], (ELEMS,), ((0, 256),), -0.2, 0.2), 1.0, 2.0)
    damage_rate = jnp.clip(jnp.exp(math.log(4.0) - 2.0794415 * jax.random.uniform(streams_of[13], (ELEMS,), jnp.float32) ** steps_of(streams_of[13], (ELEMS,), ((0, 256),), -0.2, 0.2)), 0.5, 4.0)
    return dict(dof_values=dof_values, star_matrices=star_matrices, flux_solvers=flux_solvers, stiffness=stiffness, flux_local=flux_local, flux_neighbour=flux_neighbour, flux_select=flux_select, face_source=face_source, side_list=side_list, cluster_ids=cluster_ids, damage=damage, element_size=element_size, wave_speed=wave_speed, damage_rate=damage_rate)


COURANT = 1.0
HIGHEST = lax.Precision.HIGHEST

def degree_mask():
    degrees = np.concatenate([np.full((degree + 1) * (degree + 2) // 2, degree) for degree in range(5)])
    return jnp.asarray((degrees[:, None] < degrees[None, :]).astype(np.float32))

def stress_factor(gain, quantity_count):
    stress_rows = jnp.arange(quantity_count)[:, None] < 6
    return jnp.where(stress_rows, gain[None, :], jnp.ones_like(gain)[None, :])

def star_apply(star_here, factor, field):
    applied = jnp.einsum('cqpe,pbe->cqbe', star_here, field, precision=HIGHEST)
    return applied * factor[None, :, None, :]

def derivatives(field, star_here, factor, stiffness_cut):
    series = [field]
    for power in range(4):
        applied = star_apply(star_here, factor, series[-1])
        series.append(-jnp.einsum('cij,cqje->qie', stiffness_cut, applied, precision=HIGHEST))
    return series

def taylor(series, start, stop):
    summed = jnp.zeros_like(series[0])
    factorial = 1.0
    for power in range(len(series)):
        factorial = factorial * (power + 1)
        summed = summed + (stop ** (power + 1) - start ** (power + 1)) / factorial * series[power]
    return summed

def update(integral, main_table, extra_table, weight, sources, star_here, factor, stiffness_cut, solvers, flux_local, flux_neighbour, selector):
    applied = star_apply(star_here, factor, integral)
    result = jnp.einsum('cji,cqje->qie', stiffness_cut, applied, precision=HIGHEST)
    for face_index in range(4):
        local_part = jnp.einsum('qpe,pbe->qbe', solvers[0, face_index], integral, precision=HIGHEST) * factor[:, None, :]
        result = result - jnp.einsum('ij,qje->qie', flux_local[face_index], local_part, precision=HIGHEST)
        remote_in = jnp.take(main_table, sources[face_index], axis=2)
        if extra_table is not None:
            remote_in = remote_in + weight[None, None, :] * jnp.take(extra_table, sources[face_index], axis=2)
        remote_part = jnp.einsum('qpe,pbe->qbe', solvers[1, face_index], remote_in, precision=HIGHEST) * factor[:, None, :]
        chosen = jnp.take(flux_neighbour, selector[face_index], axis=0)
        result = result - jnp.einsum('eij,qje->qie', chosen, remote_part, precision=HIGHEST)
    return result

def to_blocks(array, count):
    shaped = array.reshape(array.shape[:-1] + (count, array.shape[-1] // count))
    return jnp.moveaxis(shaped, -2, 0)

def from_blocks(blocks):
    moved_back = jnp.moveaxis(blocks, 0, -2)
    return moved_back.reshape(moved_back.shape[:-2] + (moved_back.shape[-2] * moved_back.shape[-1],))

def pick_sides(field, sides_here):
    return jnp.stack([jnp.take(field, sides_here[row], axis=2) for row in range(4)])

def halo_tables(blocks, side_blocks):
    sides = jax.vmap(pick_sides)(blocks, side_blocks)
    grid = sides.reshape((N_STRIKE, N_DEPTH) + sides.shape[1:])
    zero_strike = jnp.zeros_like(grid[:1, :, 0])
    lower_strike = jnp.concatenate([zero_strike, grid[:-1, :, 1]], axis=0)
    upper_strike = jnp.concatenate([grid[1:, :, 0], zero_strike], axis=0)
    zero_depth = jnp.zeros_like(grid[:, :1, 0])
    lower_depth = jnp.concatenate([zero_depth, grid[:, :-1, 3]], axis=1)
    upper_depth = jnp.concatenate([grid[:, 1:, 2], zero_depth], axis=1)
    parts = [piece.reshape((blocks.shape[0],) + piece.shape[2:]) for piece in (lower_strike, upper_strike, lower_depth, upper_depth)]
    return jnp.concatenate([blocks] + parts, axis=3)

def reference(dof_values, star_matrices, flux_solvers, stiffness, flux_local, flux_neighbour, flux_select, face_source, side_list, cluster_ids, damage, element_size, wave_speed, damage_rate):
    device_count = N_STRIKE * N_DEPTH
    gain = 1.0 - damage
    time_step = COURANT * jnp.min(element_size / (wave_speed * jnp.sqrt(gain)))
    stiffness_cut = stiffness * degree_mask()
    coarse = (cluster_ids != 0).astype(jnp.float32)
    factor = stress_factor(gain, Q)
    dof_b = to_blocks(dof_values, device_count)
    star_b = to_blocks(star_matrices, device_count)
    solver_b = to_blocks(flux_solvers, device_count)
    select_b = to_blocks(flux_select, device_count)
    source_b = to_blocks(face_source, device_count)
    side_b = to_blocks(side_list, device_count)
    factor_b = to_blocks(factor, device_count)
    coarse_b = to_blocks(coarse, device_count)

    def predict(inputs):
        dofs_here, star_here, factor_here = inputs
        series = derivatives(dofs_here, star_here, factor_here, stiffness_cut)
        return (taylor(series, 0.0, time_step), taylor(series, time_step, 2.0 * time_step))
    first, later = lax.map(predict, (dof_b, star_b, factor_b))
    table_a = halo_tables(first, side_b)

    def fine_step(inputs):
        dofs_here, star_here, factor_here, solver_here, select_here, source_here, table_here, first_here, later_here, coarse_here = inputs
        change = update(first_here, table_here, None, None, source_here, star_here, factor_here, stiffness_cut, solver_here, flux_local, flux_neighbour, select_here)
        is_fine = coarse_here[None, None, :] < 0.5
        middle_here = jnp.where(is_fine, dofs_here + change, dofs_here)
        series = derivatives(middle_here, star_here, factor_here, stiffness_cut)
        second_here = jnp.where(is_fine, taylor(series, 0.0, time_step), later_here)
        return (middle_here, second_here)
    middle, second = lax.map(fine_step, (dof_b, star_b, factor_b, solver_b, select_b, source_b, table_a, first, later, coarse_b))
    table_b = halo_tables(second, side_b)

    def coarse_step(inputs):
        middle_here, star_here, factor_here, solver_here, select_here, source_here, table_here, extra_here, first_here, second_here, coarse_here = inputs
        integral = second_here + coarse_here[None, None, :] * first_here
        change = update(integral, table_here, extra_here, coarse_here, source_here, star_here, factor_here, stiffness_cut, solver_here, flux_local, flux_neighbour, select_here)
        return middle_here + change
    final = lax.map(coarse_step, (middle, star_b, factor_b, solver_b, select_b, source_b, table_b, table_a, first, second, coarse_b))
    dof_next = from_blocks(final)
    first_whole = from_blocks(first)
    second_whole = from_blocks(second)
    mean_stress = (first_whole[:6, 0, :] + second_whole[:6, 0, :]) / (2.0 * time_step)
    energy = lax.optimization_barrier(jnp.sum(mean_stress * mean_stress, axis=0))
    exposure = 2.0 * time_step * damage_rate * energy / (1.0 + energy)
    new_gain = gain * jnp.exp(-exposure)
    next_step = COURANT * jnp.min(element_size / (wave_speed * jnp.sqrt(new_gain)))
    return (dof_next, 1.0 - new_gain, next_step)
```

```python
import functools

import jax
import jax.numpy as jnp
from jax import lax
from jax.experimental import pallas as pl
from jax.experimental.pallas import tpu as pltpu
from jax.sharding import PartitionSpec as P

COURANT = 1.0
Q = 9
B = 35
BP = 40
E = 128
NSEL = 48
CHUNKS = 3
PER = Q // CHUNKS
MESH = pl.DeviceIdType.MESH
f32, bf16 = jnp.float32, jnp.bfloat16
ROW_OF_SLOT = (1, 0, 3, 2)


def split(x):
    high = x.astype(bf16)
    return high, (x - high.astype(f32)).astype(bf16)


def put_stack(stack, p, x, slot):
    high, low = split(x)
    columns = pl.ds(p * E, E)
    third = 2 * slot if 3 * slot <= 128 else 128
    stack[0:slot, columns] = high
    stack[slot : 2 * slot, columns] = low
    stack[third : third + slot, columns] = high


def make_stack(matrix, slot):
    high, low = split(matrix)
    high, low = high.astype(f32), low.astype(f32)
    if 3 * slot <= 128:
        return (high + pltpu.roll(high, slot, 1) + pltpu.roll(low, 2 * slot, 1)).astype(bf16)
    return jnp.concatenate([high + pltpu.roll(high, slot, 1), low], axis=1).astype(bf16)


def degree_of(index):
    return (
        (index >= 1).astype(jnp.int32)
        + (index >= 4).astype(jnp.int32)
        + (index >= 10).astype(jnp.int32)
        + (index >= 20).astype(jnp.int32)
    )


def kernel(
    n_strike,
    n_depth,
    dof_in,
    star_in,
    solver_in,
    stiff_in,
    local_in,
    flat_in,
    select_in,
    source_in,
    side_in,
    cluster_in,
    damage_in,
    size_in,
    speed_in,
    rate_in,
    dof_out,
    damage_out,
    step_out,
    dof_raw,
    dof,
    weights,
    stiff,
    flat,
    select,
    source,
    side,
    cluster,
    damage,
    size,
    speed,
    rate,
    gather_min,
    side_got,
    first,
    later,
    second,
    middle,
    got_a,
    got_b,
    series_1,
    series_2,
    series_3,
    series_4,
    wide,
    stack,
    matrix_0,
    matrix_1,
    matrix_2,
    matrix_u,
    applied,
    own_part,
    chosen,
    pick,
    remote_a,
    remote_b,
    load_sem,
    min_send,
    min_recv,
    side_send,
    side_recv,
    halo_send,
    halo_recv,
):
    s, d = lax.axis_index("strike"), lax.axis_index("depth")

    loads = [
        pltpu.make_async_copy(src, dst, load_sem.at[index])
        for index, (src, dst) in enumerate(
            [
                (damage_in, damage),
                (size_in, size),
                (speed_in, speed),
                (stiff_in, wide.at[0:3]),
                (dof_in, dof_raw),
                (star_in, weights.at[0:3]),
                (side_in, side),
                (source_in, source),
                (select_in, select),
                (local_in, wide.at[3:7]),
                (flat_in, flat),
                (solver_in, weights.at[3:11]),
                (cluster_in, cluster),
                (rate_in, rate),
            ]
        )
    ]
    for load in loads:
        load.start()

    barrier = pltpu.get_barrier_semaphore()
    for off in range(1, n_depth):
        pl.semaphore_signal(
            barrier, inc=1, device_id={"depth": lax.rem(d + off, n_depth)}, device_id_type=MESH
        )
    for off in range(1, n_strike):
        pl.semaphore_signal(
            barrier, inc=1, device_id={"strike": lax.rem(s + off, n_strike)}, device_id_type=MESH
        )

    has = (s > 0, s < n_strike - 1, d > 0, d < n_depth - 1)
    towards = (
        (s < n_strike - 1, {"strike": lax.rem(s + 1, n_strike)}),
        (s > 0, {"strike": lax.rem(s + n_strike - 1, n_strike)}),
        (d < n_depth - 1, {"depth": lax.rem(d + 1, n_depth)}),
        (d > 0, {"depth": lax.rem(d + n_depth - 1, n_depth)}),
    )

    for load in loads[0:3]:
        load.wait()
    gain = 1.0 - damage[...]

    def min_copy(stage, me, count, axis, off):
        other = lax.rem(me + off, count)
        return pltpu.make_async_remote_copy(
            src_ref=gather_min.at[stage, me],
            dst_ref=gather_min.at[stage, me],
            send_sem=min_send.at[stage, off],
            recv_sem=min_recv.at[stage, me],
            device_id={axis: other},
            device_id_type=MESH,
        )

    def min_start(stage, row):
        me, count, axis = ((d, n_depth, "depth"), (s, n_strike, "strike"))[stage % 2]
        gather_min[stage, me] = jnp.broadcast_to(row, (8, E))
        for off in range(1, count):
            min_copy(stage, me, count, axis, off).start()

    def min_finish(stage):
        me, count, axis = ((d, n_depth, "depth"), (s, n_strike, "strike"))[stage % 2]
        for off in range(1, count):
            other = lax.rem(me + off, count)
            pltpu.make_async_remote_copy(
                src_ref=gather_min.at[stage, other],
                dst_ref=gather_min.at[stage, other],
                send_sem=min_send.at[stage, off],
                recv_sem=min_recv.at[stage, other],
                device_id={axis: other},
                device_id_type=MESH,
            ).wait_recv()
        row = gather_min[stage, 0]
        for other in range(1, count):
            row = jnp.minimum(row, gather_min[stage, other])
        return row

    def min_drain(stage):
        me, count, axis = ((d, n_depth, "depth"), (s, n_strike, "strike"))[stage % 2]
        for off in range(1, count):
            min_copy(stage, me, count, axis, off).wait_send()

    def halo_copy(which, k, chunk, where):
        rows = pl.ds(chunk * PER, PER)
        return pltpu.make_async_remote_copy(
            src_ref=(first, second)[which].at[rows],
            dst_ref=(got_a, got_b)[which].at[k, rows],
            send_sem=halo_send.at[which, k, chunk],
            recv_sem=halo_recv.at[which, k, chunk],
            device_id=where,
            device_id_type=MESH,
        )

    def side_copy(k, where):
        return pltpu.make_async_remote_copy(
            src_ref=side,
            dst_ref=side_got.at[k],
            send_sem=side_send.at[k],
            recv_sem=side_recv.at[k],
            device_id=where,
            device_id_type=MESH,
        )

    for k in range(4):

        @pl.when(jnp.logical_not(has[k]))
        def _(k=k):
            got_a[k] = jnp.zeros((Q, BP, E), f32)
            got_b[k] = jnp.zeros((Q, BP, E), f32)
            side_got[k] = jnp.full((4, E), -1, jnp.int32)

    loads[6].wait()
    pl.semaphore_wait(barrier, n_depth + n_strike - 2)
    min_start(0, size[...] / (speed[...] * jnp.sqrt(gain)))
    for k in range(4):
        exists, where = towards[k]

        @pl.when(exists)
        def _(k=k, where=where):
            side_copy(k, where).start()

    sub = lax.broadcasted_iota(jnp.int32, (BP, E), 0)
    lane = lax.broadcasted_iota(jnp.int32, (BP, E), 1)
    inside = jnp.logical_and(sub < B, lane < B)
    keep = jnp.logical_and(inside, degree_of(sub) < degree_of(lane))
    loads[3].wait()
    stiff[...] = jnp.zeros((7, E, E), f32)
    for c in range(3):
        stiff[c, 0:B, 0:B] = wide[c]
        stiff[c, 0:BP, :] = jnp.where(keep, stiff[c, 0:BP, :], 0.0)
        matrix_0[c * 24 : (c + 1) * 24, :] = stiff[c, 0:24, :]
        matrix_1[c * 16 : (c + 1) * 16, :] = jnp.where(lane[0:16] < 20, stiff[c, 0:16, :], 0.0)
        matrix_2[c * 8 : (c + 1) * 8, :] = jnp.where(lane[0:8] < 10, stiff[c, 0:8, :], 0.0)
    stack[96:128, :] = jnp.zeros((32, Q * E), bf16)
    stack[176:256, :] = jnp.zeros((80, Q * E), bf16)

    def contract(rows, block):
        def body(g, sums):
            sums = list(sums)
            for p in range(Q):
                field = block(g, p)
                for q in range(Q):
                    sums[q] = sums[q] + weights[g, q, pl.ds(p, 1), :] * field
            return tuple(sums)

        return body

    factor = [gain if q < 6 else None for q in range(Q)]

    def scaled(q, x):
        return x * factor[q] if factor[q] is not None else x

    zeros = {rows: jnp.zeros((rows, E), f32) for rows in (8, 16, 24)}

    def derive(source_rows, matrix, slot, rows, target):
        for p in range(Q):
            x = source_rows(p)
            if x.shape[0] < slot:
                x = jnp.concatenate([x, jnp.zeros((slot - x.shape[0], E), f32)], axis=0)
            put_stack(stack, p, x, slot)
        depth_rows = 256 if 3 * slot > 128 else 3 * slot
        left = make_stack(matrix, slot)[:, 0 : max(depth_rows, 128)]
        if depth_rows < 128:
            left = left[:, 0:depth_rows]
        product = jnp.dot(left, stack[0:depth_rows, :], preferred_element_type=f32)
        for c in range(3):
            for p in range(Q):
                applied[c, p, 0:rows, :] = product[c * rows : (c + 1) * rows, p * E : (p + 1) * E]
        sums = lax.fori_loop(
            0,
            3,
            contract(rows, lambda g, p: applied[g, p, 0:rows, :]),
            tuple(jnp.zeros((rows, E), f32) for _ in range(Q)),
        )
        for q in range(Q):
            target[q] = -scaled(q, sums[q])

    def taylor(base, q, weight):
        whole = weight[0] * base[q]
        low = whole[0:8] + weight[1] * series_1[q, 0:8] + weight[2] * series_2[q, 0:8]
        low = low + weight[3] * series_3[q] + weight[4] * series_4[q]
        mid = whole[8:16] + weight[1] * series_1[q, 8:16] + weight[2] * series_2[q, 8:16]
        top = whole[16:24] + weight[1] * series_1[q, 16:24]
        return jnp.concatenate([low, mid, top, whole[24:BP]], axis=0)

    loads[4].wait()
    for q in range(Q):
        dof[q, 32:BP, :] = jnp.zeros((8, E), f32)
        dof[q, 0:B, :] = dof_raw[q]
    loads[5].wait()
    derive(lambda p: dof[p], matrix_0[...], 48, 24, series_1)
    row = min_finish(0)
    min_start(1, row[0:1])
    derive(lambda p: series_1[p], matrix_1[...], 32, 16, series_2)
    derive(lambda p: series_2[p], matrix_2[...], 16, 8, series_3)
    derive(lambda p: series_3[p], matrix_2[...], 16, 8, series_4)

    loads[9].wait()
    for c in range(3):
        matrix_u[c * BP : (c + 1) * BP, :] = jnp.transpose(stiff[c])[0:BP]
    for f in range(4):
        stiff[3 + f, 0:B, 0:B] = wide[3 + f]
        matrix_u[(3 + f) * BP : (4 + f) * BP, :] = -stiff[3 + f, 0:BP, :]

    step = jnp.min(min_finish(1)[0:1], axis=1, keepdims=True) * COURANT
    step = jnp.broadcast_to(step, (1, E))
    powers, value = [], 1.0
    for power in range(5):
        value = value * step / (power + 1)
        powers.append(value)
    late = [powers[k] * (2.0 ** (k + 1) - 1.0) for k in range(5)]

    for chunk in range(CHUNKS):
        for q in range(chunk * PER, (chunk + 1) * PER):
            first[q] = taylor(dof, q, powers)
        for k in range(4):
            exists, where = towards[k]

            @pl.when(exists)
            def _(k=k, where=where, chunk=chunk):
                halo_copy(0, k, chunk, where).start()

    for q in range(Q):
        later[q] = taylor(dof, q, late)

    update_matrix = make_stack(matrix_u[...], 48)

    def own_update(source_rows):
        for p in range(Q):
            x = jnp.concatenate([source_rows(p), zeros[8]], axis=0)
            put_stack(stack, p, x, 48)
        product = jnp.dot(update_matrix, stack[...], preferred_element_type=f32)
        for g in range(7):
            for p in range(Q):
                applied[g, p] = product[g * BP : (g + 1) * BP, p * E : (p + 1) * E]
        sums = lax.fori_loop(
            0,
            7,
            contract(BP, lambda g, p: applied[g, p]),
            tuple(jnp.zeros((BP, E), f32) for _ in range(Q)),
        )
        for q in range(Q):
            own_part[q] = sums[q]

    loads[11].wait()
    own_update(lambda p: first[p])

    loads[8].wait()
    loads[10].wait()
    number = lax.rem(lax.broadcasted_iota(jnp.int32, (E, E), 0), NSEL)
    usable = lax.broadcasted_iota(jnp.int32, (E, E), 0) < 2 * NSEL
    hot = jnp.concatenate(
        [
            jnp.where(jnp.logical_and(number == select[f : f + 1, :], usable), -1.0, 0.0).astype(bf16)
            for f in range(4)
        ],
        axis=1,
    )

    def choose(index, carry):
        rows = pl.ds(pl.multiple_of(index * 200, 8), 200)
        high, low = split(flat[rows, :])
        left = (high.astype(f32) + pltpu.roll(low.astype(f32), NSEL, 1)).astype(bf16)
        product = jnp.dot(left, hot, preferred_element_type=f32)
        for f in range(4):
            chosen[f, rows, :] = product[:, f * E : (f + 1) * E]
        return carry

    lax.fori_loop(0, B * BP // 200, choose, 0)

    loads[7].wait()
    place = lax.broadcasted_iota(jnp.int32, (E, E), 0)

    def one_hot(mask):
        return jnp.where(mask, 1.0, 0.0).astype(bf16)

    for f in range(4):
        columns = slice(f * E, (f + 1) * E)
        own = one_hot(place == source[f : f + 1, :])
        pick[4, 0:E, columns] = own
        pick[4, E : 2 * E, columns] = own
    for k in range(4):

        @pl.when(has[k])
        def _(k=k):
            side_copy(k, towards[k][1]).wait_recv()

        row = ROW_OF_SLOT[k]
        left = one_hot(place == side_got[k, row : row + 1, :])
        right = jnp.concatenate(
            [one_hot(place == source[f : f + 1, :] - (E + k * E)) for f in range(4)], axis=1
        )
        picked = jnp.dot(left, right, preferred_element_type=f32).astype(bf16)
        pick[k, 0:E, :] = picked
        pick[k, E : 2 * E, :] = picked

    loads[12].wait()
    coarse = jnp.where(cluster[...] != 0, 1.0, 0.0)

    def neighbour_update(which, own_field, finish):
        blocks = (got_a, got_b)[which]
        remote = (remote_a, remote_b)[which]
        for chunk in range(CHUNKS):
            rows = slice(chunk * PER, (chunk + 1) * PER)
            for k in range(4):

                @pl.when(has[k])
                def _(k=k, chunk=chunk):
                    halo_copy(which, k, chunk, towards[k][1]).wait_recv()

            total = None
            for k in range(5):
                block = blocks[k, rows] if k < 4 else own_field[rows]
                high, low = split(block.reshape(PER * BP, E))
                left = jnp.concatenate([high, low], axis=1)
                part = jnp.dot(left, pick[k], preferred_element_type=f32)
                total = part if total is None else total + part
            for f in range(4):
                here = total[:, f * E : (f + 1) * E]
                flat_rows = slice(chunk * PER * BP, (chunk + 1) * PER * BP)
                if which == 1:
                    here = here + coarse * remote_a[f, flat_rows, :]
                remote[f, flat_rows, :] = here

            def face(f, carry, chunk=chunk):
                sums = [jnp.zeros((BP, E), f32) for _ in range(PER)]
                for j in range(B):
                    matrix = chosen[f, j * BP : (j + 1) * BP, :]
                    for n in range(PER):
                        at = (chunk * PER + n) * BP + j
                        sums[n] = sums[n] + matrix * remote[f, at : at + 1, :]
                for n in range(PER):
                    applied[7 + f, chunk * PER + n] = sums[n]
                return carry

            lax.fori_loop(0, 4, face, 0)
        sums = lax.fori_loop(
            7,
            11,
            contract(BP, lambda g, p: applied[g, p]),
            tuple(own_part[q] for q in range(Q)),
        )
        for q in range(Q):
            finish(q, scaled(q, sums[q]))

    fine = coarse < 0.5

    def finish_a(q, change):
        middle[q] = jnp.where(fine, dof[q] + change, dof[q])

    neighbour_update(0, first, finish_a)

    derive(lambda p: middle[p], matrix_0[...], 48, 24, series_1)
    derive(lambda p: series_1[p], matrix_1[...], 32, 16, series_2)
    derive(lambda p: series_2[p], matrix_2[...], 16, 8, series_3)
    derive(lambda p: series_3[p], matrix_2[...], 16, 8, series_4)
    for chunk in range(CHUNKS):
        for q in range(chunk * PER, (chunk + 1) * PER):
            second[q] = jnp.where(fine, taylor(middle, q, powers), later[q])
        for k in range(4):
            exists, where = towards[k]

            @pl.when(exists)
            def _(k=k, where=where, chunk=chunk):
                halo_copy(1, k, chunk, where).start()

    energy = jnp.zeros((1, E), f32)
    for q in range(6):
        mean = (first[q, 0:1, :] + second[q, 0:1, :]) / (2.0 * step)
        energy = energy + mean * mean
    loads[13].wait()
    exposure = 2.0 * step * rate[...] * energy / (1.0 + energy)
    new_gain = gain * jnp.exp(-exposure)
    damage_out[...] = 1.0 - new_gain
    min_start(2, size[...] / (speed[...] * jnp.sqrt(new_gain)))

    own_update(lambda p: second[p] + coarse * first[p])
    row = min_finish(2)
    min_start(3, row[0:1])

    def finish_b(q, change):
        dof_out[q] = (middle[q] + change)[0:B]

    neighbour_update(1, second, finish_b)
    step_out[...] = COURANT * jnp.min(min_finish(3)[0:1], axis=1, keepdims=True)

    for stage in range(4):
        min_drain(stage)
    for k in range(4):
        exists, where = towards[k]

        @pl.when(exists)
        def _(k=k, where=where):
            side_copy(k, where).wait_send()
            for which in range(2):
                for chunk in range(CHUNKS):
                    halo_copy(which, k, chunk, where).wait_send()


def shards(
    n_strike,
    n_depth,
    dof_values,
    star_matrices,
    flux_solvers,
    stiffness,
    flux_local,
    flux_neighbour,
    flux_select,
    face_source,
    side_list,
    cluster_ids,
    damage,
    element_size,
    wave_speed,
    damage_rate,
):
    flat = jnp.pad(jnp.transpose(flux_neighbour, (2, 1, 0)), ((0, 0), (0, BP - B), (0, E - NSEL)))
    most = max(n_strike, n_depth)
    vmem = pltpu.VMEM
    dma = pltpu.SemaphoreType.DMA
    call = pl.pallas_call(
        functools.partial(kernel, n_strike, n_depth),
        out_shape=(
            jax.ShapeDtypeStruct((Q, B, E), f32),
            jax.ShapeDtypeStruct((1, E), f32),
            jax.ShapeDtypeStruct((1, 1), f32),
        ),
        in_specs=[pl.BlockSpec(memory_space=pl.ANY)] * 14,
        out_specs=tuple(pl.BlockSpec(memory_space=pltpu.VMEM) for _ in range(3)),
        scratch_shapes=[
            vmem((Q, B, E), f32),
            vmem((Q, BP, E), f32),
            vmem((11, Q, Q, E), f32),
            vmem((7, E, E), f32),
            vmem((B * BP, E), f32),
            vmem((4, E), jnp.int32),
            vmem((4, E), jnp.int32),
            vmem((4, E), jnp.int32),
            vmem((1, E), jnp.int32),
            vmem((1, E), f32),
            vmem((1, E), f32),
            vmem((1, E), f32),
            vmem((1, E), f32),
            vmem((4, most, 8, E), f32),
            vmem((4, 4, E), jnp.int32),
            vmem((Q, BP, E), f32),
            vmem((Q, BP, E), f32),
            vmem((Q, BP, E), f32),
            vmem((Q, BP, E), f32),
            vmem((4, Q, BP, E), f32),
            vmem((4, Q, BP, E), f32),
            vmem((Q, 24, E), f32),
            vmem((Q, 16, E), f32),
            vmem((Q, 8, E), f32),
            vmem((Q, 8, E), f32),
            vmem((7, B, B), f32),
            vmem((256, Q * E), bf16),
            vmem((72, E), f32),
            vmem((48, E), f32),
            vmem((24, E), f32),
            vmem((280, E), f32),
            vmem((11, Q, BP, E), f32),
            vmem((Q, BP, E), f32),
            vmem((4, B * BP, E), f32),
            vmem((5, 2 * E, 4 * E), bf16),
            vmem((4, Q * BP, E), f32),
            vmem((4, Q * BP, E), f32),
            dma((14,)),
            dma((4, most)),
            dma((4, most)),
            dma((4,)),
            dma((4,)),
            dma((2, 4, CHUNKS)),
            dma((2, 4, CHUNKS)),
        ],
        compiler_params=pltpu.CompilerParams(
            collective_id=0, has_side_effects=True, vmem_limit_bytes=32 * 1024 * 1024
        ),
    )
    row = (1, E)
    final, new_damage, next_step = call(
        dof_values,
        star_matrices,
        flux_solvers.reshape(8, Q, Q, E),
        stiffness,
        flux_local,
        flat.reshape(B * BP, E),
        flux_select,
        face_source,
        side_list,
        cluster_ids.reshape(row),
        damage.reshape(row),
        element_size.reshape(row),
        wave_speed.reshape(row),
        damage_rate.reshape(row),
    )
    return final, new_damage.reshape(E), next_step.reshape(())


def solution(mesh):
    both = ("strike", "depth")
    in_specs = (
        P(None, None, both),
        P(None, None, None, both),
        P(None, None, None, None, both),
        P(),
        P(),
        P(),
        P(None, both),
        P(None, both),
        P(None, both),
        P(both),
        P(both),
        P(both),
        P(both),
        P(both),
    )
    out_specs = (P(None, None, both), P(both), P())
    body = functools.partial(shards, mesh.shape["strike"], mesh.shape["depth"])
    return jax.shard_map(body, mesh=mesh, in_specs=in_specs, out_specs=out_specs, check_vma=False)
```

```python
import functools

import jax
import jax.numpy as jnp
from jax import lax
from jax.experimental import pallas as pl
from jax.experimental.pallas import tpu as pltpu
from jax.sharding import PartitionSpec as P

COURANT = 1.0
Q = 9
B = 35
BP = 40
E = 128
HALF = 64
NSEL = 48
MESH = pl.DeviceIdType.MESH
f32, bf16 = jnp.float32, jnp.bfloat16
ROW_OF_SLOT = (1, 0, 3, 2)
TERMS = ((0, 0, 35), (1, 0, 20), (1, 24, 10), (1, 20, 4), (1, 34, 1))
MARK = 35
ROWS = (40, 24, 16, 8, 8)
SLOTS = (48, 32, 16, 16, 16)


def split(x):
    high = x.astype(bf16)
    return high, (x - high.astype(f32)).astype(bf16)


def third_of(slot):
    return 2 * slot if 3 * slot <= 128 else 128


def make_stack(matrix, slot):
    lane = lax.broadcasted_iota(jnp.int32, matrix.shape, 1)
    high, low = split(jnp.where(lane < slot, matrix, 0.0))
    high, low = high.astype(f32), low.astype(f32)
    if 3 * slot <= 128:
        return (high + pltpu.roll(high, slot, 1) + pltpu.roll(low, 2 * slot, 1)).astype(bf16)
    return jnp.concatenate([high + pltpu.roll(high, slot, 1), low], axis=1).astype(bf16)


def degree_of(index):
    degree = jnp.zeros_like(index)
    for first in (1, 4, 10, 20):
        degree = degree + jnp.where(index >= first, 1, 0)
    return degree


def kernel(
    n_strike,
    n_depth,
    dof_in,
    star_in,
    solver_in,
    stiff_in,
    local_in,
    flat_in,
    select_in,
    source_in,
    side_in,
    cluster_in,
    damage_in,
    size_in,
    speed_in,
    rate_in,
    dof_out,
    damage_out,
    step_out,
    dof_raw,
    star,
    solver,
    wide_stiff,
    wide_local,
    wide_flat,
    select,
    source,
    side,
    cluster,
    damage,
    size,
    speed,
    rate,
    minima,
    side_got,
    sent_a,
    sent_b,
    got_a,
    got_b,
    series_1,
    series_2,
    series_3,
    series_4,
    first,
    second,
    middle,
    stiff,
    flat,
    fine_weights,
    stack,
    matrix_0,
    matrix_1,
    matrix_2,
    matrix_u,
    applied,
    part,
    chosen,
    pick,
    gathered,
    remote,
    load_sem,
    min_send,
    min_recv,
    side_send,
    side_recv,
    halo_send,
    halo_recv,
):
    s, d = lax.axis_index("strike"), lax.axis_index("depth")
    series = (sent_a.at[0], series_1, series_2, series_3, series_4)

    loads = [
        pltpu.make_async_copy(src, dst, load_sem.at[index])
        for index, (src, dst) in enumerate(
            [
                (damage_in, damage),
                (size_in, size),
                (speed_in, speed),
                (dof_in, dof_raw),
                (cluster_in, cluster),
                (stiff_in, wide_stiff),
                (star_in, star),
                (side_in, side),
                (solver_in, solver),
                (local_in, wide_local),
                (flat_in, wide_flat),
                (select_in, select),
                (source_in, source),
                (rate_in, rate),
            ]
        )
    ]

    barrier = pltpu.get_barrier_semaphore()
    groups = {"depth": (d, n_depth), "strike": (s, n_strike)}
    order = sorted(range(1, max(n_depth, n_strike)), key=lambda off: abs(off - n_depth / 2))
    for off in order:
        for axis, (me, count) in groups.items():
            if off < count:
                pl.semaphore_signal(
                    barrier, inc=1, device_id={axis: lax.rem(me + off, count)}, device_id_type=MESH
                )
    for load in loads:
        load.start()

    has = (s > 0, s < n_strike - 1, d > 0, d < n_depth - 1)
    towards = (
        (s < n_strike - 1, {"strike": lax.rem(s + 1, n_strike)}),
        (s > 0, {"strike": lax.rem(s + n_strike - 1, n_strike)}),
        (d < n_depth - 1, {"depth": lax.rem(d + 1, n_depth)}),
        (d > 0, {"depth": lax.rem(d + n_depth - 1, n_depth)}),
    )

    def min_copy(stage, slot, off):
        axis = ("depth", "strike")[stage % 2]
        me, count = groups[axis]
        return pltpu.make_async_remote_copy(
            src_ref=minima.at[stage, slot],
            dst_ref=minima.at[stage, slot],
            send_sem=min_send.at[stage, off],
            recv_sem=min_recv.at[stage, slot],
            device_id={axis: lax.rem(me + off, count)},
            device_id_type=MESH,
        )

    def min_offsets(stage):
        count = groups[("depth", "strike")[stage % 2]][1]
        return [off for off in order if off < count]

    def min_start(stage, row):
        me, count = groups[("depth", "strike")[stage % 2]]
        minima[stage, me] = row
        for off in min_offsets(stage):
            min_copy(stage, me, off).start()

    def min_finish(stage):
        me, count = groups[("depth", "strike")[stage % 2]]
        for off in reversed(min_offsets(stage)):
            min_copy(stage, lax.rem(me + off, count), off).wait_recv()
        rows = [minima[stage, other] for other in range(count)]
        while len(rows) > 1:
            rows = [jnp.minimum(a, b) for a, b in zip(rows[::2], rows[1::2])] + rows[len(rows) // 2 * 2 :]
        return rows[0]

    def min_drain(stage):
        me, _ = groups[("depth", "strike")[stage % 2]]
        for off in min_offsets(stage):
            min_copy(stage, me, off).wait_send()

    def halo_copy(piece, k, where):
        return pltpu.make_async_remote_copy(
            src_ref=sent_a.at[piece] if piece < 2 else sent_b,
            dst_ref=got_a.at[k, piece] if piece < 2 else got_b.at[k],
            send_sem=halo_send.at[piece, k],
            recv_sem=halo_recv.at[piece, k],
            device_id=where,
            device_id_type=MESH,
        )

    def side_copy(k, where):
        return pltpu.make_async_remote_copy(
            src_ref=side,
            dst_ref=side_got.at[k],
            send_sem=side_send.at[k],
            recv_sem=side_recv.at[k],
            device_id=where,
            device_id_type=MESH,
        )

    def to_all(send):
        for k in range(4):
            exists, where = towards[k]

            @pl.when(exists)
            def _(k=k, where=where):
                send(k, where)

    def from_all(receive):
        for k in range(4):

            @pl.when(has[k])
            def _(k=k):
                receive(k, towards[k][1])

    for k in range(4):

        @pl.when(jnp.logical_not(has[k]))
        def _(k=k):
            got_a[k] = jnp.zeros((2, Q, BP, E), f32)
            got_b[k] = jnp.zeros((5, BP, E), f32)
            side_got[k] = jnp.full((4, E), -1, jnp.int32)

    stack[96:128, :] = jnp.zeros((32, Q * E), bf16)
    stack[176:256, :] = jnp.zeros((80, Q * E), bf16)
    stiff[...] = jnp.zeros((7, E, E), f32)

    left_half = lax.broadcasted_iota(jnp.int32, (BP, E), 1) < HALF
    left_row = left_half[0:1]
    sub = lax.broadcasted_iota(jnp.int32, (BP, E), 0)
    lane = lax.broadcasted_iota(jnp.int32, (BP, E), 1)

    def swap(x):
        return pltpu.roll(x, HALF, 1)

    def twice(x):
        return jnp.where(left_half[0 : x.shape[0]], x, swap(x))

    for load in loads[0:3]:
        load.wait()
    gain = 1.0 - damage[...]
    own_ratio = size[...] / (speed[...] * jnp.sqrt(gain))

    loads[3].wait()
    loads[4].wait()
    coarse = jnp.where(cluster[...] != 0, 1.0, 0.0)
    for q in range(Q):
        sent_a[0, q, 32:BP, :] = jnp.zeros((8, E), f32)
        sent_a[0, q, 0:B, :] = dof_raw[q]
    sent_a[0, 0, MARK : MARK + 1, :] = coarse

    loads[5].wait()
    inside = jnp.logical_and(sub < B, lane < B)
    keep = jnp.logical_and(inside, degree_of(sub) < degree_of(lane))
    for c in range(3):
        stiff[c, 0:B, 0:B] = wide_stiff[c]
        kept = jnp.where(keep, stiff[c, 0:BP, :], 0.0)
        stiff[c, 0:BP, :] = kept
        matrix_0[c * 24 : (c + 1) * 24, :] = kept[0:24]
        matrix_1[c * 16 : (c + 1) * 16, :] = jnp.where(lane[0:16] < 20, kept[0:16], 0.0)
        matrix_2[c * 8 : (c + 1) * 8, :] = jnp.where(lane[0:8] < 10, kept[0:8], 0.0)

    def put_stack(source_rows, slot):
        third = third_of(slot)
        for p in range(Q):
            x = source_rows(p)
            if x.shape[0] < slot:
                x = jnp.concatenate([x, jnp.zeros((slot - x.shape[0], E), f32)], axis=0)
            high, low = split(x)
            columns = pl.ds(p * E, E)
            stack[0:slot, columns] = high
            stack[slot : 2 * slot, columns] = low
            stack[third : third + slot, columns] = high

    def stacked_dot(left, slot):
        rows = 256 if 3 * slot > 128 else 3 * slot
        return jnp.dot(left[:, 0:rows], stack[0:rows, :], preferred_element_type=f32)

    def contract(weight, pieces, rows, sums):
        def body(p, sums):
            sums = list(sums)
            for g in pieces:
                field = applied[g, p, 0:rows, :]
                for q in range(Q):
                    sums[q] = sums[q] + weight(q, p, g) * field
            return tuple(sums)

        return lax.fori_loop(0, Q, body, tuple(sums))

    def nothing(rows):
        return [jnp.zeros((rows, E), f32) for _ in range(Q)]

    def scaled(q, x, by):
        return x * by if q < 6 else x

    def star_weight(q, p, c):
        return star[q, p, c : c + 1, :]

    def fine_weight(shift):
        return lambda q, p, g: fine_weights[q, p, g + shift : g + shift + 1, :]

    def derive(source_rows, order_in, target, fine):
        matrix = (matrix_0, matrix_1, matrix_2, matrix_2)[order_in]
        rows, slot = (24, 16, 8, 8)[order_in], SLOTS[order_in]
        put_stack(source_rows, slot)
        product = stacked_dot(make_stack(matrix[...], slot), slot)
        for p in range(Q):
            pieces = [product[c * rows : (c + 1) * rows, p * E : (p + 1) * E] for c in range(3)]
            if fine:
                pieces = [jnp.where(left_half[0:rows], pieces[0], pieces[1]), pieces[2]]
            for g, piece in enumerate(pieces):
                applied[g, p, 0:rows, :] = piece
        if fine:
            sums = contract(fine_weight(0), range(2), rows, nothing(rows))
        else:
            sums = contract(star_weight, range(3), rows, nothing(rows))
        for q in range(Q):
            total = sums[q] + swap(sums[q]) if fine else sums[q]
            target[q] = -scaled(q, total, gain_fine if fine else gain)

    loads[6].wait()
    for index in range(4):
        derive(lambda p, index=index: series[index][p], index, series[index + 1], False)
    for q in range(Q):
        sent_a[1, q, 0:16, :] = series_1[q, 0:16]
        sent_a[1, q, 16:24, :] = series_1[q, 16:24] + pltpu.roll(series_3[q], 4, 0)
        sent_a[1, q, 24:32, :] = series_2[q, 0:8]
        sent_a[1, q, 32:40, :] = series_2[q, 8:16] + pltpu.roll(series_4[q], 2, 0)

    loads[7].wait()
    pl.semaphore_wait(barrier, n_depth + n_strike - 2)
    min_start(0, own_ratio)
    to_all(lambda k, where: side_copy(k, where).start())
    for piece in range(2):
        to_all(lambda k, where: halo_copy(piece, k, where).start())

    loads[8].wait()

    def pack(q, carry):
        for p in range(Q):
            rows = [star[q, p, c : c + 1, :] for c in range(3)]
            own = [solver[0, q, p, f : f + 1, :] for f in range(4)]
            other = [solver[1, q, p, f : f + 1, :] for f in range(4)]
            tile = [
                jnp.where(left_row, rows[0], swap(rows[1])),
                jnp.where(left_row, rows[2], 0.0),
                jnp.where(left_row, own[0], swap(own[1])),
                jnp.where(left_row, own[2], swap(own[3])),
                jnp.where(left_row, other[0], swap(other[1])),
                jnp.where(left_row, other[2], swap(other[3])),
                jnp.where(left_row, swap(other[0]), other[1]),
                jnp.where(left_row, swap(other[2]), other[3]),
            ]
            for r in range(8):
                fine_weights[q, p, r : r + 1, :] = tile[r]
        return carry

    lax.fori_loop(0, Q, pack, 0)
    gain_fine = twice(gain)

    loads[9].wait()
    for c in range(3):
        matrix_u[c * BP : (c + 1) * BP, :] = jnp.transpose(stiff[c])[0:BP]
    for f in range(4):
        stiff[3 + f, 0:B, 0:B] = wide_local[:, f, :]
        matrix_u[(3 + f) * BP : (4 + f) * BP, :] = -stiff[3 + f, 0:BP, :]

    def own_fine(k):
        put_stack(lambda p: twice(series[k][p]), SLOTS[k])
        product = stacked_dot(make_stack(matrix_u[...], SLOTS[k]), SLOTS[k])
        for p in range(Q):
            pieces = [product[g * BP : (g + 1) * BP, p * E : (p + 1) * E] for g in range(7)]
            applied[0, p] = jnp.where(left_half, pieces[0], pieces[1])
            applied[1, p] = pieces[2]
            applied[2, p] = jnp.where(left_half, pieces[3], pieces[4])
            applied[3, p] = jnp.where(left_half, pieces[5], pieces[6])
        sums = contract(fine_weight(0), range(4), BP, nothing(BP))
        for q in range(Q):
            part[k, q] = sums[q]

    own_fine(0)
    own_fine(1)
    own_fine(2)
    row = min_finish(0)
    min_start(1, row)
    own_fine(3)
    own_fine(4)

    def paired(ref):
        rows = [ref[f : f + 1, :] for f in range(4)]
        return [
            jnp.where(left_row, rows[0], swap(rows[1])),
            jnp.where(left_row, rows[2], swap(rows[3])),
            jnp.where(left_row, swap(rows[0]), rows[1]),
            jnp.where(left_row, swap(rows[2]), rows[3]),
        ]

    loads[11].wait()
    number = lax.rem(lax.broadcasted_iota(jnp.int32, (E, E), 0), NSEL)
    usable = lax.broadcasted_iota(jnp.int32, (E, E), 0) < 2 * NSEL
    hot = jnp.concatenate(
        [
            jnp.where(jnp.logical_and(number == row, usable), -1.0, 0.0).astype(bf16)
            for row in paired(select)
        ],
        axis=1,
    )
    loads[10].wait()
    flat[...] = jnp.zeros((B * BP, E), f32)

    def clear(j, carry):
        for g in range(4):
            chosen[g, pl.ds(pl.multiple_of(j * BP + 32, 8), 8), :] = jnp.zeros((8, E), f32)
        return carry

    lax.fori_loop(0, B, clear, 0)

    def choose(index, carry):
        for n in range(5):
            flat[pl.ds(pl.multiple_of((index * 5 + n) * BP, 8), B), 0:NSEL] = wide_flat[index * 5 + n]
        high, low = split(flat[pl.ds(pl.multiple_of(index * 200, 8), 200), :])
        left = (high.astype(f32) + pltpu.roll(low.astype(f32), NSEL, 1)).astype(bf16)
        product = jnp.dot(left, hot, preferred_element_type=f32)
        for n in range(5):
            for g in range(4):
                chosen[g, pl.ds(index * 5 + n, B, stride=BP), :] = product[
                    n * BP : n * BP + B, g * E : (g + 1) * E
                ]
        return carry

    lax.fori_loop(0, 7, choose, 0)

    loads[12].wait()
    place = lax.broadcasted_iota(jnp.int32, (E, E), 0)

    def one_hot(mask):
        return jnp.where(mask, 1.0, 0.0).astype(bf16)

    sources = paired(source)
    from_all(lambda k, where: side_copy(k, where).wait_recv())
    for k in range(5):
        right = jnp.concatenate([one_hot(place == row - (E + k * E) % (5 * E)) for row in sources], axis=1)
        if k < 4:
            row = ROW_OF_SLOT[k]
            left = one_hot(place == side_got[k, row : row + 1, :])
            right = jnp.dot(left, right, preferred_element_type=f32).astype(bf16)
        pick[k, 0:E, :] = right
        pick[k, E : 2 * E, :] = right

    def gather(blocks):
        total = None
        for k in range(5):
            high, low = split(blocks[k])
            left = jnp.concatenate([high, low], axis=1)
            value = jnp.dot(left, pick[k], preferred_element_type=f32)
            total = value if total is None else total + value
        return total

    for piece in range(2):
        from_all(lambda k, where: halo_copy(piece, k, where).wait_recv())
        for chunk in range(3):
            rows = slice(3 * chunk, 3 * chunk + 3)
            total = gather(
                [got_a[k, piece, rows].reshape(3 * BP, E) for k in range(4)]
                + [sent_a[piece, rows].reshape(3 * BP, E)]
            )
            for g in range(4):
                gathered[piece, g, chunk * 3 * BP : (chunk + 1) * 3 * BP, :] = total[:, g * E : (g + 1) * E]

    def near(source_row, count, g, row):
        sums = nothing(BP)
        for j in range(count):
            matrix = chosen[g, j * BP : (j + 1) * BP, :]
            for p in range(Q):
                sums[p] = sums[p] + matrix * source_row(p, j)
        for p in range(Q):
            applied[row, p] = sums[p]

    for k in range(5):
        block, start, count = TERMS[k]

        def face(g, carry, block=block, start=start, count=count):
            near(lambda p, j: gathered[block, g, pl.ds(p * BP + start + j, 1), :], count, g, 4 + g)
            return carry

        lax.fori_loop(0, 2, face, 0)
        sums = contract(fine_weight(0), range(4, 6), BP, [part[k, q] for q in range(Q)])
        for q in range(Q):
            part[k, q] = sums[q]

    step = jnp.min(min_finish(1), axis=1, keepdims=True) * COURANT
    step = jnp.broadcast_to(step, (1, E))
    powers, value = [], 1.0
    for power in range(5):
        value = value * step / (power + 1)
        powers.append(value)
    late = [powers[k] * (2.0 ** (k + 1) - 1.0) for k in range(5)]

    def taylor(base, q, weight):
        whole = weight[0] * base[q]
        low = whole[0:8] + weight[1] * series_1[q, 0:8] + weight[2] * series_2[q, 0:8]
        low = low + weight[3] * series_3[q] + weight[4] * series_4[q]
        mid = whole[8:16] + weight[1] * series_1[q, 8:16] + weight[2] * series_2[q, 8:16]
        top = whole[16:24] + weight[1] * series_1[q, 16:24]
        return jnp.concatenate([low, mid, top, whole[24:BP]], axis=0)

    fine = coarse < 0.5
    for q in range(Q):
        first[q] = taylor(sent_a.at[0], q, powers)
        second[q] = taylor(sent_a.at[0], q, late)
        change = powers[0] * part[0, q]
        for k in range(1, 5):
            change = change + powers[k] * part[k, q]
        change = change + swap(change)
        middle[q] = twice(sent_a[0, q]) + scaled(q, change, gain_fine)
    for index in range(4):
        base = middle if index == 0 else series[index]
        derive(lambda p, base=base: base[p], index, series[index + 1], True)
    fine_left = jnp.logical_and(fine, left_row)
    for q in range(Q):
        applied[10, q] = taylor(middle, q, powers)
    for q in range(Q):
        second[q] = jnp.where(fine_left, applied[10, q], second[q])

    energy = jnp.zeros((1, E), f32)
    for q in range(6):
        mean = (first[q, 0:1, :] + second[q, 0:1, :]) / (2.0 * step)
        energy = energy + mean * mean
    loads[13].wait()
    exposure = 2.0 * step * rate[...] * energy / (1.0 + energy)
    new_gain = gain * jnp.exp(-exposure)
    min_start(2, size[...] / (speed[...] * jnp.sqrt(new_gain)))
    damage_out[...] = 1.0 - new_gain

    fine_both = twice(jnp.where(fine, 1.0, 0.0))
    for n in range(5):
        other = applied[10, 2 * n + 1] if n < 4 else jnp.zeros((BP, E), f32)
        sent_b[n] = jnp.where(left_half, applied[10, 2 * n], other) * fine_both
    to_all(lambda k, where: halo_copy(2, k, where).start())

    put_stack(lambda p: second[p] + coarse * first[p], 48)
    product = stacked_dot(make_stack(matrix_u[...], 48), 48)
    for g in range(7):
        for p in range(Q):
            applied[g, p] = product[g * BP : (g + 1) * BP, p * E : (p + 1) * E]

    def own_weight(q, p, g):
        return star[q, p, g : g + 1, :] if g < 3 else solver[0, q, p, g - 3 : g - 2, :]

    sums = contract(own_weight, range(7), BP, nothing(BP))
    for q in range(Q):
        part[0, q] = sums[q]
    for q in range(Q):
        base = jnp.where(fine_left, middle[q], sent_a[0, q])
        middle[q] = base

    coarse_halves = [
        jnp.where(left_row, coarse, swap(coarse)),
        jnp.where(left_row, swap(coarse), coarse),
    ]
    sub8 = lax.broadcasted_iota(jnp.int32, (8, E), 0)
    for g in range(4):
        theirs = gathered[0, g, MARK : MARK + 1, :]
        weight = [late[k] * theirs + powers[k] * coarse_halves[g // 2] for k in range(5)]
        for p in range(Q):
            low = [gathered[0, g, p * BP + 8 * t : p * BP + 8 * t + 8, :] for t in range(5)]
            high = [gathered[1, g, p * BP + 8 * t : p * BP + 8 * t + 8, :] for t in range(5)]
            value = [weight[0] * x for x in low]
            d_3 = jnp.where(sub8 < 4, pltpu.roll(high[2], 4, 0), 0.0)
            d_4 = jnp.where(sub8 < 1, pltpu.roll(high[4], 6, 0), 0.0)
            value[0] = value[0] + weight[1] * high[0] + weight[2] * high[3] + weight[3] * d_3 + weight[4] * d_4
            value[1] = value[1] + weight[1] * high[1] + weight[2] * jnp.where(sub8 < 2, high[4], 0.0)
            value[2] = value[2] + weight[1] * jnp.where(sub8 < 4, high[2], 0.0)
            for t in range(5):
                remote[g, p * BP + 8 * t : p * BP + 8 * t + 8, :] = value[t]

    for k in range(5):
        pick[k, HALF:E, :] = jnp.zeros((HALF, 4 * E), bf16)
        pick[k, E + HALF : 2 * E, :] = jnp.zeros((HALF, 4 * E), bf16)

    row = min_finish(2)
    min_start(3, row)
    from_all(lambda k, where: halo_copy(2, k, where).wait_recv())
    for n in range(5):
        blocks = [got_b[k, n] for k in range(4)] + [sent_b[n]]
        total = gather([jnp.concatenate([x, swap(x)], axis=0) for x in blocks])
        for half in range(2 if n < 4 else 1):
            rows = slice((2 * n + half) * BP, (2 * n + half + 1) * BP)
            for g in range(4):
                value = total[half * BP : (half + 1) * BP, g * E : (g + 1) * E]
                remote[g, rows, :] = remote[g, rows, :] + value

    def last_face(g, carry):
        near(lambda p, j: remote[g, p * BP + j : p * BP + j + 1, :], B, g, g)
        return carry

    lax.fori_loop(0, 4, last_face, 0)
    left_sums = contract(fine_weight(4), range(2), BP, nothing(BP))
    for q in range(Q):
        total = left_sums[q]
        part[1, q] = total + swap(total)
    right_sums = contract(fine_weight(4), range(2, 4), BP, nothing(BP))
    for q in range(Q):
        total = right_sums[q]
        value = part[0, q] + jnp.where(left_half, part[1, q], total + swap(total))
        dof_out[q] = (middle[q] + scaled(q, value, gain))[0:B]

    step_out[...] = COURANT * jnp.min(min_finish(3), axis=1, keepdims=True)

    for stage in range(4):
        min_drain(stage)

    def drain(k, where):
        side_copy(k, where).wait_send()
        for piece in range(3):
            halo_copy(piece, k, where).wait_send()

    to_all(drain)


def shards(
    n_strike,
    n_depth,
    dof_values,
    star_matrices,
    flux_solvers,
    stiffness,
    flux_local,
    flux_neighbour,
    flux_select,
    face_source,
    side_list,
    cluster_ids,
    damage,
    element_size,
    wave_speed,
    damage_rate,
):
    most = max(n_strike, n_depth)
    vmem = pltpu.VMEM
    dma = pltpu.SemaphoreType.DMA
    call = pl.pallas_call(
        functools.partial(kernel, n_strike, n_depth),
        out_shape=(
            jax.ShapeDtypeStruct((Q, B, E), f32),
            jax.ShapeDtypeStruct((1, E), f32),
            jax.ShapeDtypeStruct((1, 1), f32),
        ),
        in_specs=[pl.BlockSpec(memory_space=pltpu.HBM)] * 14,
        out_specs=tuple(pl.BlockSpec(memory_space=pltpu.VMEM) for _ in range(3)),
        scratch_shapes=[
            vmem((Q, B, E), f32),
            vmem((Q, Q, 3, E), f32),
            vmem((2, Q, Q, 4, E), f32),
            vmem((3, B, B), f32),
            vmem((B, 4, B), f32),
            vmem((B, B, NSEL), f32),
            vmem((4, E), jnp.int32),
            vmem((4, E), jnp.int32),
            vmem((4, E), jnp.int32),
            vmem((1, E), jnp.int32),
            vmem((1, E), f32),
            vmem((1, E), f32),
            vmem((1, E), f32),
            vmem((1, E), f32),
            vmem((4, most, 1, E), f32),
            vmem((4, 4, E), jnp.int32),
            vmem((2, Q, BP, E), f32),
            vmem((5, BP, E), f32),
            vmem((4, 2, Q, BP, E), f32),
            vmem((4, 5, BP, E), f32),
            vmem((Q, 24, E), f32),
            vmem((Q, 16, E), f32),
            vmem((Q, 8, E), f32),
            vmem((Q, 8, E), f32),
            vmem((Q, BP, E), f32),
            vmem((Q, BP, E), f32),
            vmem((Q, BP, E), f32),
            vmem((7, E, E), f32),
            vmem((B * BP, E), f32),
            vmem((Q, Q, 8, E), f32),
            vmem((256, Q * E), bf16),
            vmem((72, E), f32),
            vmem((48, E), f32),
            vmem((24, E), f32),
            vmem((280, E), f32),
            vmem((11, Q, BP, E), f32),
            vmem((5, Q, BP, E), f32),
            vmem((4, B * BP, E), f32),
            vmem((5, 2 * E, 4 * E), bf16),
            vmem((2, 4, Q * BP, E), f32),
            vmem((4, Q * BP, E), f32),
            dma((14,)),
            dma((4, most)),
            dma((4, most)),
            dma((4,)),
            dma((4,)),
            dma((3, 4)),
            dma((3, 4)),
        ],
        compiler_params=pltpu.CompilerParams(
            collective_id=0, has_side_effects=True, vmem_limit_bytes=32 * 1024 * 1024
        ),
    )
    row = (1, E)
    final, new_damage, next_step = call(
        dof_values,
        jnp.transpose(star_matrices, (1, 2, 0, 3)),
        jnp.transpose(flux_solvers, (0, 2, 3, 1, 4)),
        stiffness,
        jnp.transpose(flux_local, (1, 0, 2)),
        jnp.transpose(flux_neighbour, (1, 2, 0)),
        flux_select,
        face_source,
        side_list,
        cluster_ids.reshape(row),
        damage.reshape(row),
        element_size.reshape(row),
        wave_speed.reshape(row),
        damage_rate.reshape(row),
    )
    return final, new_damage.reshape(E), next_step.reshape(())


def solution(mesh):
    both = ("strike", "depth")
    in_specs = (
        P(None, None, both),
        P(None, None, None, both),
        P(None, None, None, None, both),
        P(),
        P(),
        P(),
        P(None, both),
        P(None, both),
        P(None, both),
        P(both),
        P(both),
        P(both),
        P(both),
        P(both),
    )
    out_specs = (P(None, None, both), P(both), P())
    body = functools.partial(shards, mesh.shape["strike"], mesh.shape["depth"])
    return jax.shard_map(body, mesh=mesh, in_specs=in_specs, out_specs=out_specs, check_vma=False)
```

```python
import functools

import jax
import jax.numpy as jnp
from jax import lax
from jax.experimental import pallas as pl
from jax.experimental.pallas import tpu as pltpu
from jax.sharding import PartitionSpec as P

COURANT = 1.0
Q = 9
B = 35
BP = 40
E = 128
HALF = 64
NSEL = 48
MESH = pl.DeviceIdType.MESH
f32, bf16 = jnp.float32, jnp.bfloat16
ROW_OF_SLOT = (1, 0, 3, 2)
TERMS = ((0, 0, 35), (1, 0, 20), (1, 24, 10), (1, 20, 4), (1, 34, 1))
MARK = 35
ROWS = (40, 24, 16, 8, 8)
SLOTS = (48, 32, 16, 16, 16)


def split(x):
    high = x.astype(bf16)
    return high, (x - high.astype(f32)).astype(bf16)


def third_of(slot):
    return 2 * slot if 3 * slot <= 128 else 128


def make_stack(matrix, slot):
    lane = lax.broadcasted_iota(jnp.int32, matrix.shape, 1)
    high, low = split(jnp.where(lane < slot, matrix, 0.0))
    high, low = high.astype(f32), low.astype(f32)
    if 3 * slot <= 128:
        return (high + pltpu.roll(high, slot, 1) + pltpu.roll(low, 2 * slot, 1)).astype(bf16)
    return jnp.concatenate([high + pltpu.roll(high, slot, 1), low], axis=1).astype(bf16)


def degree_of(index):
    degree = jnp.zeros_like(index)
    for first in (1, 4, 10, 20):
        degree = degree + jnp.where(index >= first, 1, 0)
    return degree


def kernel(
    n_strike,
    n_depth,
    dof_in,
    star_in,
    solver_in,
    stiff_in,
    local_in,
    flat_in,
    select_in,
    source_in,
    side_in,
    cluster_in,
    damage_in,
    size_in,
    speed_in,
    rate_in,
    dof_out,
    damage_out,
    step_out,
    dof_raw,
    star,
    solver,
    wide_stiff,
    wide_local,
    wide_flat,
    select,
    source,
    side,
    cluster,
    damage,
    size,
    speed,
    rate,
    minima,
    side_got,
    sent_a,
    sent_b,
    got_a,
    got_b,
    series_1,
    series_2,
    series_3,
    series_4,
    first,
    second,
    middle,
    stiff,
    flat,
    fine_weights,
    stack,
    matrix_0,
    matrix_1,
    matrix_2,
    matrix_u,
    applied,
    part,
    chosen,
    pick,
    gathered,
    remote,
    load_sem,
    min_send,
    min_recv,
    side_send,
    side_recv,
    halo_send,
    halo_recv,
):
    s, d = lax.axis_index("strike"), lax.axis_index("depth")
    series = (sent_a.at[0], series_1, series_2, series_3, series_4)

    loads = [
        pltpu.make_async_copy(src, dst, load_sem.at[index])
        for index, (src, dst) in enumerate(
            [
                (damage_in, damage),
                (size_in, size),
                (speed_in, speed),
                (dof_in, dof_raw),
                (cluster_in, cluster),
                (stiff_in, wide_stiff),
                (star_in, star),
                (side_in, side),
                (solver_in, solver),
                (local_in, wide_local),
                (flat_in, wide_flat),
                (select_in, select),
                (source_in, source),
                (rate_in, rate),
            ]
        )
    ]

    barrier = pltpu.get_barrier_semaphore()
    groups = {"depth": (d, n_depth), "strike": (s, n_strike)}
    order = sorted(range(1, max(n_depth, n_strike)), key=lambda off: abs(off - n_depth / 2))
    for off in order:
        for axis, (me, count) in groups.items():
            if off < count:
                pl.semaphore_signal(
                    barrier, inc=1, device_id={axis: lax.rem(me + off, count)}, device_id_type=MESH
                )
    for load in loads:
        load.start()

    has = (s > 0, s < n_strike - 1, d > 0, d < n_depth - 1)
    towards = (
        (s < n_strike - 1, {"strike": lax.rem(s + 1, n_strike)}),
        (s > 0, {"strike": lax.rem(s + n_strike - 1, n_strike)}),
        (d < n_depth - 1, {"depth": lax.rem(d + 1, n_depth)}),
        (d > 0, {"depth": lax.rem(d + n_depth - 1, n_depth)}),
    )

    def min_copy(stage, slot, off):
        axis = ("strike", "depth")[stage % 2]
        me, count = groups[axis]
        return pltpu.make_async_remote_copy(
            src_ref=minima.at[stage, slot],
            dst_ref=minima.at[stage, slot],
            send_sem=min_send.at[stage, off],
            recv_sem=min_recv.at[stage, slot],
            device_id={axis: lax.rem(me + off, count)},
            device_id_type=MESH,
        )

    def min_offsets(stage):
        count = groups[("strike", "depth")[stage % 2]][1]
        return [off for off in order if off < count]

    def min_start(stage, row):
        me, count = groups[("strike", "depth")[stage % 2]]
        minima[stage, me] = row
        for off in min_offsets(stage):
            min_copy(stage, me, off).start()

    def min_finish(stage):
        me, count = groups[("strike", "depth")[stage % 2]]
        for off in reversed(min_offsets(stage)):
            min_copy(stage, lax.rem(me + off, count), off).wait_recv()
        rows = [minima[stage, other] for other in range(count)]
        while len(rows) > 1:
            rows = [jnp.minimum(a, b) for a, b in zip(rows[::2], rows[1::2])] + rows[len(rows) // 2 * 2 :]
        return rows[0]

    def min_drain(stage):
        me, _ = groups[("strike", "depth")[stage % 2]]
        for off in min_offsets(stage):
            min_copy(stage, me, off).wait_send()

    def halo_copy(piece, k, where):
        return pltpu.make_async_remote_copy(
            src_ref=sent_a.at[piece] if piece < 2 else sent_b,
            dst_ref=got_a.at[k, piece] if piece < 2 else got_b.at[k],
            send_sem=halo_send.at[piece, k],
            recv_sem=halo_recv.at[piece, k],
            device_id=where,
            device_id_type=MESH,
        )

    def side_copy(k, where):
        return pltpu.make_async_remote_copy(
            src_ref=side,
            dst_ref=side_got.at[k],
            send_sem=side_send.at[k],
            recv_sem=side_recv.at[k],
            device_id=where,
            device_id_type=MESH,
        )

    def to_all(send):
        for k in range(4):
            exists, where = towards[k]

            @pl.when(exists)
            def _(k=k, where=where):
                send(k, where)

    def from_all(receive):
        for k in range(4):

            @pl.when(has[k])
            def _(k=k):
                receive(k, towards[k][1])

    for k in range(4):

        @pl.when(jnp.logical_not(has[k]))
        def _(k=k):
            got_a[k] = jnp.zeros((2, Q, BP, E), f32)
            got_b[k] = jnp.zeros((5, BP, E), f32)
            side_got[k] = jnp.full((4, E), -1, jnp.int32)

    stack[96:128, :] = jnp.zeros((32, Q * E), bf16)
    stack[176:256, :] = jnp.zeros((80, Q * E), bf16)
    stiff[...] = jnp.zeros((7, E, E), f32)

    left_half = lax.broadcasted_iota(jnp.int32, (BP, E), 1) < HALF
    left_row = left_half[0:1]
    sub = lax.broadcasted_iota(jnp.int32, (BP, E), 0)
    lane = lax.broadcasted_iota(jnp.int32, (BP, E), 1)

    def swap(x):
        return pltpu.roll(x, HALF, 1)

    def twice(x):
        return jnp.where(left_half[0 : x.shape[0]], x, swap(x))

    for load in loads[0:3]:
        load.wait()
    gain = 1.0 - damage[...]
    own_ratio = size[...] / (speed[...] * jnp.sqrt(gain))

    loads[3].wait()
    loads[4].wait()
    coarse = jnp.where(cluster[...] != 0, 1.0, 0.0)
    for q in range(Q):
        sent_a[0, q, 32:BP, :] = jnp.zeros((8, E), f32)
        sent_a[0, q, 0:B, :] = dof_raw[q]
    sent_a[0, 0, MARK : MARK + 1, :] = coarse

    loads[5].wait()
    inside = jnp.logical_and(sub < B, lane < B)
    keep = jnp.logical_and(inside, degree_of(sub) < degree_of(lane))
    for c in range(3):
        stiff[c, 0:B, 0:B] = wide_stiff[c]
        kept = jnp.where(keep, stiff[c, 0:BP, :], 0.0)
        stiff[c, 0:BP, :] = kept
        matrix_0[c * 24 : (c + 1) * 24, :] = kept[0:24]
        matrix_1[c * 16 : (c + 1) * 16, :] = jnp.where(lane[0:16] < 20, kept[0:16], 0.0)
        matrix_2[c * 8 : (c + 1) * 8, :] = jnp.where(lane[0:8] < 10, kept[0:8], 0.0)

    def put_stack(source_rows, slot):
        third = third_of(slot)
        for p in range(Q):
            x = source_rows(p)
            if x.shape[0] < slot:
                x = jnp.concatenate([x, jnp.zeros((slot - x.shape[0], E), f32)], axis=0)
            high, low = split(x)
            columns = pl.ds(p * E, E)
            stack[0:slot, columns] = high
            stack[slot : 2 * slot, columns] = low
            stack[third : third + slot, columns] = high

    def stacked_dot(left, slot):
        rows = 256 if 3 * slot > 128 else 3 * slot
        return jnp.dot(left[:, 0:rows], stack[0:rows, :], preferred_element_type=f32)

    def contract(weight, pieces, rows, sums):
        def body(p, sums):
            sums = list(sums)
            for g in pieces:
                field = applied[g, p, 0:rows, :]
                for q in range(Q):
                    sums[q] = sums[q] + weight(q, p, g) * field
            return tuple(sums)

        if rows <= 16:
            for p in range(Q):
                sums = body(p, sums)
            return sums
        return lax.fori_loop(0, Q, body, tuple(sums))

    def nothing(rows):
        return [jnp.zeros((rows, E), f32) for _ in range(Q)]

    def scaled(q, x, by):
        return x * by if q < 6 else x

    def star_weight(q, p, c):
        return star[q, p, c : c + 1, :]

    def fine_weight(shift):
        return lambda q, p, g: fine_weights[q, p, g + shift : g + shift + 1, :]

    def derive(source_rows, order_in, target, fine):
        matrix = (matrix_0, matrix_1, matrix_2, matrix_2)[order_in]
        rows, slot = (24, 16, 8, 8)[order_in], SLOTS[order_in]
        put_stack(source_rows, slot)
        product = stacked_dot(make_stack(matrix[...], slot), slot)
        for p in range(Q):
            pieces = [product[c * rows : (c + 1) * rows, p * E : (p + 1) * E] for c in range(3)]
            if fine:
                pieces = [jnp.where(left_half[0:rows], pieces[0], pieces[1]), pieces[2]]
            for g, piece in enumerate(pieces):
                applied[g, p, 0:rows, :] = piece
        if fine:
            sums = contract(fine_weight(0), range(2), rows, nothing(rows))
        else:
            sums = contract(star_weight, range(3), rows, nothing(rows))
        for q in range(Q):
            total = sums[q] + swap(sums[q]) if fine else sums[q]
            target[q] = -scaled(q, total, gain_fine if fine else gain)

    loads[6].wait()
    for index in range(4):
        derive(lambda p, index=index: series[index][p], index, series[index + 1], False)
    for q in range(Q):
        sent_a[1, q, 0:16, :] = series_1[q, 0:16]
        sent_a[1, q, 16:24, :] = series_1[q, 16:24] + pltpu.roll(series_3[q], 4, 0)
        sent_a[1, q, 24:32, :] = series_2[q, 0:8]
        sent_a[1, q, 32:40, :] = series_2[q, 8:16] + pltpu.roll(series_4[q], 2, 0)

    loads[8].wait()

    def pack(q, carry):
        for p in range(Q):
            rows = [star[q, p, c : c + 1, :] for c in range(3)]
            own = [solver[0, q, p, f : f + 1, :] for f in range(4)]
            other = [solver[1, q, p, f : f + 1, :] for f in range(4)]
            tile = [
                jnp.where(left_row, rows[0], swap(rows[1])),
                jnp.where(left_row, rows[2], 0.0),
                jnp.where(left_row, own[0], swap(own[1])),
                jnp.where(left_row, own[2], swap(own[3])),
                jnp.where(left_row, other[0], swap(other[1])),
                jnp.where(left_row, other[2], swap(other[3])),
                jnp.where(left_row, swap(other[0]), other[1]),
                jnp.where(left_row, swap(other[2]), other[3]),
            ]
            for r in range(8):
                fine_weights[q, p, r : r + 1, :] = tile[r]
        return carry

    lax.fori_loop(0, Q, pack, 0)
    gain_fine = twice(gain)

    loads[9].wait()
    for c in range(3):
        matrix_u[c * BP : (c + 1) * BP, :] = jnp.transpose(stiff[c])[0:BP]
    for f in range(4):
        stiff[3 + f, 0:B, 0:B] = wide_local[:, f, :]
        matrix_u[(3 + f) * BP : (4 + f) * BP, :] = -stiff[3 + f, 0:BP, :]

    def own_fine(k):
        put_stack(lambda p: twice(series[k][p]), SLOTS[k])
        product = stacked_dot(make_stack(matrix_u[...], SLOTS[k]), SLOTS[k])
        for p in range(Q):
            pieces = [product[g * BP : (g + 1) * BP, p * E : (p + 1) * E] for g in range(7)]
            applied[0, p] = jnp.where(left_half, pieces[0], pieces[1])
            applied[1, p] = pieces[2]
            applied[2, p] = jnp.where(left_half, pieces[3], pieces[4])
            applied[3, p] = jnp.where(left_half, pieces[5], pieces[6])
        sums = contract(fine_weight(0), range(4), BP, nothing(BP))
        for q in range(Q):
            part[k, q] = sums[q]

    own_fine(0)
    loads[7].wait()
    pl.semaphore_wait(barrier, n_depth + n_strike - 2)
    min_start(0, own_ratio)
    to_all(lambda k, where: side_copy(k, where).start())
    for piece in range(2):
        to_all(lambda k, where: halo_copy(piece, k, where).start())

    for k in range(1, 5):
        own_fine(k)

    def paired(ref):
        rows = [ref[f : f + 1, :] for f in range(4)]
        return [
            jnp.where(left_row, rows[0], swap(rows[1])),
            jnp.where(left_row, rows[2], swap(rows[3])),
            jnp.where(left_row, swap(rows[0]), rows[1]),
            jnp.where(left_row, swap(rows[2]), rows[3]),
        ]

    loads[12].wait()
    place = lax.broadcasted_iota(jnp.int32, (E, E), 0)

    def one_hot(mask):
        return jnp.where(mask, 1.0, 0.0).astype(bf16)

    sources = paired(source)
    from_all(lambda k, where: side_copy(k, where).wait_recv())
    for k in range(5):
        right = jnp.concatenate([one_hot(place == row - (E + k * E) % (5 * E)) for row in sources], axis=1)
        if k < 4:
            row = ROW_OF_SLOT[k]
            left = one_hot(place == side_got[k, row : row + 1, :])
            right = jnp.dot(left, right, preferred_element_type=f32).astype(bf16)
        pick[k, 0:E, :] = right
        pick[k, E : 2 * E, :] = right

    row = min_finish(0)
    min_start(1, row)

    loads[11].wait()
    number = lax.rem(lax.broadcasted_iota(jnp.int32, (E, E), 0), NSEL)
    usable = lax.broadcasted_iota(jnp.int32, (E, E), 0) < 2 * NSEL
    hot = jnp.concatenate(
        [
            jnp.where(jnp.logical_and(number == row, usable), -1.0, 0.0).astype(bf16)
            for row in paired(select)
        ],
        axis=1,
    )
    loads[10].wait()
    flat[...] = jnp.zeros((B * BP, E), f32)

    def clear(j, carry):
        for g in range(4):
            chosen[g, pl.ds(pl.multiple_of(j * BP + 32, 8), 8), :] = jnp.zeros((8, E), f32)
        return carry

    lax.fori_loop(0, B, clear, 0)

    def choose(index, carry):
        for n in range(5):
            flat[pl.ds(pl.multiple_of((index * 5 + n) * BP, 8), B), 0:NSEL] = wide_flat[index * 5 + n]
        high, low = split(flat[pl.ds(pl.multiple_of(index * 200, 8), 200), :])
        left = (high.astype(f32) + pltpu.roll(low.astype(f32), NSEL, 1)).astype(bf16)
        product = jnp.dot(left, hot, preferred_element_type=f32)
        for n in range(5):
            for g in range(4):
                chosen[g, pl.ds(index * 5 + n, B, stride=BP), :] = product[
                    n * BP : n * BP + B, g * E : (g + 1) * E
                ]
        return carry

    lax.fori_loop(0, 7, choose, 0)

    def gather(blocks, columns):
        total = None
        for k in range(5):
            high, low = split(blocks[k])
            left = jnp.concatenate([high, low], axis=1)
            value = jnp.dot(left, pick[k, :, columns], preferred_element_type=f32)
            total = value if total is None else total + value
        return total

    def gather_series(piece, half):
        for chunk in range(3):
            rows = slice(3 * chunk, 3 * chunk + 3)
            total = gather(
                [got_a[k, piece, rows].reshape(3 * BP, E) for k in range(4)]
                + [sent_a[piece, rows].reshape(3 * BP, E)],
                slice(2 * half * E, 2 * half * E + 2 * E),
            )
            for g in range(2):
                place = slice(chunk * 3 * BP, (chunk + 1) * 3 * BP)
                gathered[piece, 2 * half + g, place, :] = total[:, g * E : (g + 1) * E]

    def near(source_row, count, g, row):
        sums = nothing(BP)
        for j in range(count):
            matrix = chosen[g, j * BP : (j + 1) * BP, :]
            for p in range(Q):
                sums[p] = sums[p] + matrix * source_row(p, j)
        for p in range(Q):
            applied[row, p] = sums[p]

    for k in range(5):
        block, start, count = TERMS[k]
        if k < 2:
            from_all(lambda k, where: halo_copy(block, k, where).wait_recv())
            gather_series(block, 0)

        def face(g, carry, k=k, block=block, start=start, count=count):
            near(lambda p, j: gathered[block, g, pl.ds(p * BP + start + j, 1), :], count, g, 2 * k + g)
            return carry

        lax.fori_loop(0, 2, face, 0)

    step = jnp.min(min_finish(1), axis=1, keepdims=True) * COURANT
    step = jnp.broadcast_to(step, (1, E))
    powers, value = [], 1.0
    for power in range(5):
        value = value * step / (power + 1)
        powers.append(value)
    late = [powers[k] * (2.0 ** (k + 1) - 1.0) for k in range(5)]

    def taylor(base, q, weight):
        whole = weight[0] * base[q]
        low = whole[0:8] + weight[1] * series_1[q, 0:8] + weight[2] * series_2[q, 0:8]
        low = low + weight[3] * series_3[q] + weight[4] * series_4[q]
        mid = whole[8:16] + weight[1] * series_1[q, 8:16] + weight[2] * series_2[q, 8:16]
        top = whole[16:24] + weight[1] * series_1[q, 16:24]
        return jnp.concatenate([low, mid, top, whole[24:BP]], axis=0)

    fine = coarse < 0.5
    for q in range(Q):
        first[q] = taylor(sent_a.at[0], q, powers)
        second[q] = taylor(sent_a.at[0], q, late)
    for p in range(Q):
        for g in range(2):
            value = powers[0] * applied[g, p]
            for k in range(1, 5):
                value = value + powers[k] * applied[2 * k + g, p]
            applied[g, p] = value
    changes = []
    for q in range(Q):
        value = powers[0] * part[0, q]
        for k in range(1, 5):
            value = value + powers[k] * part[k, q]
        changes.append(value)
    changes = contract(fine_weight(4), range(2), BP, changes)
    for q in range(Q):
        change = changes[q] + swap(changes[q])
        middle[q] = twice(sent_a[0, q]) + scaled(q, change, gain_fine)
    for index in range(4):
        base = middle if index == 0 else series[index]
        derive(lambda p, base=base: base[p], index, series[index + 1], True)
    fine_left = jnp.logical_and(fine, left_row)
    for q in range(Q):
        applied[10, q] = taylor(middle, q, powers)
        second[q] = jnp.where(fine_left, applied[10, q], second[q])

    energy = jnp.zeros((1, E), f32)
    for q in range(6):
        mean = (first[q, 0:1, :] + second[q, 0:1, :]) / (2.0 * step)
        energy = energy + mean * mean
    loads[13].wait()
    exposure = 2.0 * step * rate[...] * energy / (1.0 + energy)
    new_gain = gain * jnp.exp(-exposure)
    min_start(2, size[...] / (speed[...] * jnp.sqrt(new_gain)))
    damage_out[...] = 1.0 - new_gain

    fine_both = twice(jnp.where(fine, 1.0, 0.0))
    for n in range(5):
        other = applied[10, 2 * n + 1] if n < 4 else jnp.zeros((BP, E), f32)
        sent_b[n] = jnp.where(left_half, applied[10, 2 * n], other) * fine_both
    to_all(lambda k, where: halo_copy(2, k, where).start())

    put_stack(lambda p: second[p] + coarse * first[p], 48)
    product = stacked_dot(make_stack(matrix_u[...], 48), 48)
    for g in range(7):
        for p in range(Q):
            applied[g, p] = product[g * BP : (g + 1) * BP, p * E : (p + 1) * E]

    def own_weight(q, p, g):
        return star[q, p, g : g + 1, :] if g < 3 else solver[0, q, p, g - 3 : g - 2, :]

    sums = contract(own_weight, range(7), BP, nothing(BP))
    for q in range(Q):
        part[0, q] = sums[q]
    for q in range(Q):
        base = jnp.where(fine_left, middle[q], sent_a[0, q])
        middle[q] = base

    for piece in range(2):
        gather_series(piece, 1)

    coarse_halves = [
        jnp.where(left_row, coarse, swap(coarse)),
        jnp.where(left_row, swap(coarse), coarse),
    ]
    sub8 = lax.broadcasted_iota(jnp.int32, (8, E), 0)
    for g in range(4):
        theirs = gathered[0, g, MARK : MARK + 1, :]
        weight = [late[k] * theirs + powers[k] * coarse_halves[g // 2] for k in range(5)]
        for p in range(Q):
            low = [gathered[0, g, p * BP + 8 * t : p * BP + 8 * t + 8, :] for t in range(5)]
            high = [gathered[1, g, p * BP + 8 * t : p * BP + 8 * t + 8, :] for t in range(5)]
            value = [weight[0] * x for x in low]
            d_3 = jnp.where(sub8 < 4, pltpu.roll(high[2], 4, 0), 0.0)
            d_4 = jnp.where(sub8 < 1, pltpu.roll(high[4], 6, 0), 0.0)
            value[0] = value[0] + weight[1] * high[0] + weight[2] * high[3] + weight[3] * d_3 + weight[4] * d_4
            value[1] = value[1] + weight[1] * high[1] + weight[2] * jnp.where(sub8 < 2, high[4], 0.0)
            value[2] = value[2] + weight[1] * jnp.where(sub8 < 4, high[2], 0.0)
            for t in range(5):
                remote[g, p * BP + 8 * t : p * BP + 8 * t + 8, :] = value[t]

    for k in range(5):
        pick[k, HALF:E, :] = jnp.zeros((HALF, 4 * E), bf16)
        pick[k, E + HALF : 2 * E, :] = jnp.zeros((HALF, 4 * E), bf16)

    row = min_finish(2)
    min_start(3, row)
    from_all(lambda k, where: halo_copy(2, k, where).wait_recv())
    for n in range(5):
        blocks = [got_b[k, n] for k in range(4)] + [sent_b[n]]
        total = gather([jnp.concatenate([x, swap(x)], axis=0) for x in blocks], slice(0, 4 * E))
        for half in range(2 if n < 4 else 1):
            rows = slice((2 * n + half) * BP, (2 * n + half + 1) * BP)
            for g in range(4):
                value = total[half * BP : (half + 1) * BP, g * E : (g + 1) * E]
                remote[g, rows, :] = remote[g, rows, :] + value

    def last_face(g, carry):
        near(lambda p, j: remote[g, p * BP + j : p * BP + j + 1, :], B, g, g)
        return carry

    lax.fori_loop(0, 4, last_face, 0)
    left_sums = contract(fine_weight(4), range(2), BP, nothing(BP))
    for q in range(Q):
        total = left_sums[q]
        part[1, q] = total + swap(total)
    right_sums = contract(fine_weight(4), range(2, 4), BP, nothing(BP))
    for q in range(Q):
        total = right_sums[q]
        value = part[0, q] + jnp.where(left_half, part[1, q], total + swap(total))
        dof_out[q] = (middle[q] + scaled(q, value, gain))[0:B]

    step_out[...] = COURANT * jnp.min(min_finish(3), axis=1, keepdims=True)

    for stage in range(4):
        min_drain(stage)

    def drain(k, where):
        side_copy(k, where).wait_send()
        for piece in range(3):
            halo_copy(piece, k, where).wait_send()

    to_all(drain)


def shards(
    n_strike,
    n_depth,
    dof_values,
    star_matrices,
    flux_solvers,
    stiffness,
    flux_local,
    flux_neighbour,
    flux_select,
    face_source,
    side_list,
    cluster_ids,
    damage,
    element_size,
    wave_speed,
    damage_rate,
):
    out_shape = (
        jax.ShapeDtypeStruct((Q, B, E), f32),
        jax.ShapeDtypeStruct((1, E), f32),
        jax.ShapeDtypeStruct((1, 1), f32),
    )
    most = max(n_strike, n_depth)
    vmem = pltpu.VMEM
    dma = pltpu.SemaphoreType.DMA
    call = pl.pallas_call(
        functools.partial(kernel, n_strike, n_depth),
        out_shape=out_shape,
        in_specs=[pl.BlockSpec(memory_space=pltpu.HBM)] * 14,
        out_specs=tuple(pl.BlockSpec(memory_space=pltpu.VMEM) for _ in range(3)),
        scratch_shapes=[
            vmem((Q, B, E), f32),
            vmem((Q, Q, 3, E), f32),
            vmem((2, Q, Q, 4, E), f32),
            vmem((3, B, B), f32),
            vmem((B, 4, B), f32),
            vmem((B, B, NSEL), f32),
            vmem((4, E), jnp.int32),
            vmem((4, E), jnp.int32),
            vmem((4, E), jnp.int32),
            vmem((1, E), jnp.int32),
            vmem((1, E), f32),
            vmem((1, E), f32),
            vmem((1, E), f32),
            vmem((1, E), f32),
            vmem((4, most, 1, E), f32),
            vmem((4, 4, E), jnp.int32),
            vmem((2, Q, BP, E), f32),
            vmem((5, BP, E), f32),
            vmem((4, 2, Q, BP, E), f32),
            vmem((4, 5, BP, E), f32),
            vmem((Q, 24, E), f32),
            vmem((Q, 16, E), f32),
            vmem((Q, 8, E), f32),
            vmem((Q, 8, E), f32),
            vmem((Q, BP, E), f32),
            vmem((Q, BP, E), f32),
            vmem((Q, BP, E), f32),
            vmem((7, E, E), f32),
            vmem((B * BP, E), f32),
            vmem((Q, Q, 8, E), f32),
            vmem((256, Q * E), bf16),
            vmem((72, E), f32),
            vmem((48, E), f32),
            vmem((24, E), f32),
            vmem((280, E), f32),
            vmem((11, Q, BP, E), f32),
            vmem((5, Q, BP, E), f32),
            vmem((4, B * BP, E), f32),
            vmem((5, 2 * E, 4 * E), bf16),
            vmem((2, 4, Q * BP, E), f32),
            vmem((4, Q * BP, E), f32),
            dma((14,)),
            dma((4, most)),
            dma((4, most)),
            dma((4,)),
            dma((4,)),
            dma((3, 4)),
            dma((3, 4)),
        ],
        compiler_params=pltpu.CompilerParams(
            collective_id=0, has_side_effects=True, vmem_limit_bytes=32 * 1024 * 1024
        ),
    )
    row = (1, E)
    operands = (
        dof_values,
        jnp.transpose(star_matrices, (1, 2, 0, 3)),
        jnp.transpose(flux_solvers, (0, 2, 3, 1, 4)),
        stiffness,
        jnp.transpose(flux_local, (1, 0, 2)),
        jnp.transpose(flux_neighbour, (1, 2, 0)),
        flux_select,
        face_source,
        side_list,
        cluster_ids.reshape(row),
        damage.reshape(row),
        element_size.reshape(row),
        wave_speed.reshape(row),
        damage_rate.reshape(row),
    )
    final, new_damage, next_step = call(
        *(pltpu.with_memory_space_constraint(x, pltpu.HBM) for x in operands)
    )
    return final, new_damage.reshape(E), next_step.reshape(())


def solution(mesh):
    both = ("strike", "depth")
    in_specs = (
        P(None, None, both),
        P(None, None, None, both),
        P(None, None, None, None, both),
        P(),
        P(),
        P(),
        P(None, both),
        P(None, both),
        P(None, both),
        P(both),
        P(both),
        P(both),
        P(both),
        P(both),
    )
    out_specs = (P(None, None, both), P(both), P())
    body = functools.partial(shards, mesh.shape["strike"], mesh.shape["depth"])
    return jax.shard_map(body, mesh=mesh, in_specs=in_specs, out_specs=out_specs, check_vma=False)
```

```python
import functools

import jax
import jax.numpy as jnp
from jax import lax
from jax.experimental import pallas as pl
from jax.experimental.pallas import tpu as pltpu
from jax.sharding import PartitionSpec as P

COURANT = 1.0
Q = 9
B = 35
BP = 40
E = 128
HALF = 64
NSEL = 48
MESH = pl.DeviceIdType.MESH
f32, bf16 = jnp.float32, jnp.bfloat16
ROW_OF_SLOT = (1, 0, 3, 2)
START, HEIGHT = (0, 32), (32, 40)
SENT = 72
MARK = 38
CHUNKS = 1
PER = Q // CHUNKS
STAGES = ("strike", "depth", "depth", "strike")
LAST = ((0, 5),)
ROWS = (40, 24, 16, 8, 8)
SLOTS = (48, 32, 16, 16, 16)


def split(x):
    high = x.astype(bf16)
    return high, (x - high.astype(f32)).astype(bf16)


def third_of(slot):
    return 2 * slot if 3 * slot <= 128 else 128


def make_stack(matrix, slot):
    lane = lax.broadcasted_iota(jnp.int32, matrix.shape, 1)
    high, low = split(jnp.where(lane < slot, matrix, 0.0))
    high, low = high.astype(f32), low.astype(f32)
    if 3 * slot <= 128:
        return (high + pltpu.roll(high, slot, 1) + pltpu.roll(low, 2 * slot, 1)).astype(bf16)
    return jnp.concatenate([high + pltpu.roll(high, slot, 1), low], axis=1).astype(bf16)


def degree_of(index):
    degree = jnp.zeros_like(index)
    for first in (1, 4, 10, 20):
        degree = degree + jnp.where(index >= first, 1, 0)
    return degree


def kernel(
    n_strike,
    n_depth,
    dof_in,
    star_in,
    solver_in,
    stiff_in,
    local_in,
    flat_in,
    select_in,
    source_in,
    side_in,
    cluster_in,
    damage_in,
    size_in,
    speed_in,
    rate_in,
    dof_out,
    damage_out,
    step_out,
    dof_raw,
    star,
    solver,
    wide_stiff,
    wide_local,
    wide_flat,
    select,
    source,
    side,
    cluster,
    damage,
    size,
    speed,
    rate,
    minima,
    side_got,
    dof,
    sent,
    sent_b,
    got,
    got_b,
    series_1,
    series_2,
    series_3,
    series_4,
    first,
    second,
    middle,
    stiff,
    flat,
    fine_weights,
    stack,
    matrix_0,
    matrix_1,
    matrix_2,
    matrix_u,
    applied,
    face_terms,
    part,
    chosen,
    pick,
    gathered_0,
    gathered_1,
    remote,
    load_sem,
    min_send,
    min_recv,
    side_send,
    side_recv,
    halo_send,
    halo_recv,
):
    s, d = lax.axis_index("strike"), lax.axis_index("depth")
    gathered = (gathered_0, gathered_1)
    series = (dof, series_1, series_2, series_3, series_4)

    loads = [
        pltpu.make_async_copy(src, dst, load_sem.at[index])
        for index, (src, dst) in enumerate(
            [
                (damage_in, damage),
                (size_in, size),
                (speed_in, speed),
                (dof_in, dof_raw),
                (side_in, side),
                (stiff_in, wide_stiff),
                (star_in, star),
                (cluster_in, cluster),
                (solver_in, solver),
                (local_in, wide_local),
                (flat_in, wide_flat),
                (select_in, select),
                (source_in, source),
                (rate_in, rate),
            ]
        )
    ]

    barrier = pltpu.get_barrier_semaphore()
    groups = {"depth": (d, n_depth), "strike": (s, n_strike)}
    order = sorted(range(1, max(n_depth, n_strike)), key=lambda off: abs(off - n_depth / 2))
    for off in order:
        for axis, (me, count) in groups.items():
            if off < count:
                pl.semaphore_signal(
                    barrier, inc=1, device_id={axis: lax.rem(me + off, count)}, device_id_type=MESH
                )
    for load in loads:
        load.start()

    has = (s > 0, s < n_strike - 1, d > 0, d < n_depth - 1)
    towards = (
        (s < n_strike - 1, {"strike": lax.rem(s + 1, n_strike)}),
        (s > 0, {"strike": lax.rem(s + n_strike - 1, n_strike)}),
        (d < n_depth - 1, {"depth": lax.rem(d + 1, n_depth)}),
        (d > 0, {"depth": lax.rem(d + n_depth - 1, n_depth)}),
    )

    def min_copy(stage, slot, off):
        axis = STAGES[stage]
        me, count = groups[axis]
        return pltpu.make_async_remote_copy(
            src_ref=minima.at[stage, slot],
            dst_ref=minima.at[stage, slot],
            send_sem=min_send.at[stage, off],
            recv_sem=min_recv.at[stage, slot],
            device_id={axis: lax.rem(me + off, count)},
            device_id_type=MESH,
        )

    def min_offsets(stage):
        count = groups[STAGES[stage]][1]
        return [off for off in order if off < count]

    def min_start(stage, row):
        me, count = groups[STAGES[stage]]
        minima[stage, me] = row
        for off in min_offsets(stage):
            min_copy(stage, me, off).start()

    def min_finish(stage):
        me, count = groups[STAGES[stage]]
        for off in reversed(min_offsets(stage)):
            min_copy(stage, lax.rem(me + off, count), off).wait_recv()
        rows = [minima[stage, other] for other in range(count)]
        while len(rows) > 1:
            rows = [jnp.minimum(a, b) for a, b in zip(rows[::2], rows[1::2])] + rows[len(rows) // 2 * 2 :]
        return rows[0]

    def min_drain(stage):
        me, _ = groups[STAGES[stage]]
        for off in min_offsets(stage):
            min_copy(stage, me, off).wait_send()

    def halo_copy(piece, chunk, k, where):
        if piece < 2:
            rows = pl.ds(chunk * PER, PER)
            height = pl.ds(START[piece], HEIGHT[piece])
            src, dst = sent.at[rows, height], got.at[k, rows, height]
        else:
            rows = pl.ds(LAST[chunk][0], LAST[chunk][1] - LAST[chunk][0])
            src, dst = sent_b.at[rows], got_b.at[k, rows]
        return pltpu.make_async_remote_copy(
            src_ref=src,
            dst_ref=dst,
            send_sem=halo_send.at[piece, chunk, k],
            recv_sem=halo_recv.at[piece, chunk, k],
            device_id=where,
            device_id_type=MESH,
        )

    def side_copy(k, where):
        return pltpu.make_async_remote_copy(
            src_ref=side,
            dst_ref=side_got.at[k],
            send_sem=side_send.at[k],
            recv_sem=side_recv.at[k],
            device_id=where,
            device_id_type=MESH,
        )

    def to_all(send, ks=range(4)):
        for k in ks:
            exists, where = towards[k]

            @pl.when(exists)
            def _(k=k, where=where):
                send(k, where)

    def from_all(receive):
        for k in range(4):

            @pl.when(has[k])
            def _(k=k):
                receive(k, towards[k][1])

    left_half = lax.broadcasted_iota(jnp.int32, (BP, E), 1) < HALF
    left_row = left_half[0:1]
    sub = lax.broadcasted_iota(jnp.int32, (BP, E), 0)
    lane = lax.broadcasted_iota(jnp.int32, (BP, E), 1)

    def swap(x):
        return pltpu.roll(x, HALF, 1)

    def twice(x):
        return jnp.where(left_half[0 : x.shape[0]], x, swap(x))

    for load in loads[0:3]:
        load.wait()
    gain = 1.0 - damage[...]
    own_ratio = size[...] / (speed[...] * jnp.sqrt(gain))
    pl.semaphore_wait(barrier, n_depth + n_strike - 2)
    min_start(0, own_ratio)
    loads[3].wait()
    for q in range(Q):
        sent[q, 0:32, :] = dof_raw[q, 0:32, :]
    for ks in ((0, 1), (2, 3)):
        for chunk in range(CHUNKS):
            to_all(lambda k, where: halo_copy(0, chunk, k, where).start(), ks)
    loads[4].wait()
    to_all(lambda k, where: side_copy(k, where).start())

    for k in range(4):

        @pl.when(jnp.logical_not(has[k]))
        def _(k=k):
            got[k] = jnp.zeros((Q, SENT, E), f32)
            got_b[k] = jnp.zeros((5, BP, E), f32)
            side_got[k] = jnp.full((4, E), -1, jnp.int32)

    stack[96:128, :] = jnp.zeros((32, Q * E), bf16)
    stack[176:256, :] = jnp.zeros((80, Q * E), bf16)
    stiff[...] = jnp.zeros((7, E, E), f32)

    loads[7].wait()
    coarse = jnp.where(cluster[...] != 0, 1.0, 0.0)
    for q in range(Q):
        dof[q, 32:BP, :] = jnp.zeros((8, E), f32)
        dof[q, 0:B, :] = dof_raw[q]

    loads[5].wait()
    inside = jnp.logical_and(sub < B, lane < B)
    keep = jnp.logical_and(inside, degree_of(sub) < degree_of(lane))
    for c in range(3):
        stiff[c, 0:B, 0:B] = wide_stiff[c]
        kept = jnp.where(keep, stiff[c, 0:BP, :], 0.0)
        stiff[c, 0:BP, :] = kept
        matrix_0[c * 24 : (c + 1) * 24, :] = kept[0:24]
        matrix_1[c * 16 : (c + 1) * 16, :] = jnp.where(lane[0:16] < 20, kept[0:16], 0.0)
        matrix_2[c * 8 : (c + 1) * 8, :] = jnp.where(lane[0:8] < 10, kept[0:8], 0.0)

    def put_stack(source_rows, slot):
        third = third_of(slot)
        for p in range(Q):
            x = source_rows(p)
            if x.shape[0] < slot:
                x = jnp.concatenate([x, jnp.zeros((slot - x.shape[0], E), f32)], axis=0)
            high, low = split(x)
            columns = pl.ds(p * E, E)
            stack[0:slot, columns] = high
            stack[slot : 2 * slot, columns] = low
            stack[third : third + slot, columns] = high

    def stacked_dot(left, slot):
        rows = 256 if 3 * slot > 128 else 3 * slot
        return jnp.dot(left[:, 0:rows], stack[0:rows, :], preferred_element_type=f32)

    def contract(weight, pieces, rows, sums):
        def body(p, sums):
            sums = list(sums)
            for g in pieces:
                field = applied[g, p, 0:rows, :]
                for q in range(Q):
                    sums[q] = sums[q] + weight(q, p, g) * field
            return tuple(sums)

        if rows <= 16:
            for p in range(Q):
                sums = body(p, sums)
            return sums
        return lax.fori_loop(0, Q, body, tuple(sums))

    def nothing(rows):
        return [jnp.zeros((rows, E), f32) for _ in range(Q)]

    def scaled(q, x, by):
        return x * by if q < 6 else x

    def star_weight(q, p, c):
        return star[q, p, c : c + 1, :]

    pack_rows = (16, 18, 0, 2, 4, 6, 12, 14)

    def fine_weight(shift):
        def weight(q, p, g):
            row = pack_rows[g + shift]
            return fine_weights[q, p, row : row + 1, :]

        return weight

    def derive(source_rows, order_in, target, fine):
        matrix = (matrix_0, matrix_1, matrix_2, matrix_2)[order_in]
        rows, slot = (24, 16, 8, 8)[order_in], SLOTS[order_in]
        put_stack(source_rows, slot)
        product = stacked_dot(make_stack(matrix[...], slot), slot)
        for p in range(Q):
            pieces = [product[c * rows : (c + 1) * rows, p * E : (p + 1) * E] for c in range(3)]
            if fine:
                pieces = [jnp.where(left_half[0:rows], pieces[0], pieces[1]), pieces[2]]
            for g, piece in enumerate(pieces):
                applied[g, p, 0:rows, :] = piece
        if fine:
            sums = contract(fine_weight(0), range(2), rows, nothing(rows))
        else:
            sums = contract(star_weight, range(3), rows, nothing(rows))
        for q in range(Q):
            total = sums[q] + swap(sums[q]) if fine else sums[q]
            target[q] = -scaled(q, total, gain_fine if fine else gain)

    loads[6].wait()
    for index in range(4):
        derive(lambda p, index=index: series[index][p], index, series[index + 1], False)
    sub8 = lax.broadcasted_iota(jnp.int32, (8, E), 0)
    for q in range(Q):
        turned = pltpu.roll(series_2[q, 0:8], 4, 0)
        sent[q, 32:40, :] = (
            dof[q, 32:BP, :] + pltpu.roll(series_3[q], 3, 0) + pltpu.roll(series_4[q], 7, 0)
        )
        sent[q, 40:56, :] = series_1[q, 0:16]
        sent[q, 56:64, :] = series_1[q, 16:24] + jnp.where(sub8 >= 4, turned, 0.0)
        sent[q, 64:72, :] = jnp.where(sub8 < 4, turned, 0.0) + pltpu.roll(series_2[q, 8:16], 4, 0)
    sent[0, 32 + MARK : 33 + MARK, :] = coarse
    for ks in ((0, 1), (2, 3)):
        for chunk in range(CHUNKS):
            to_all(lambda k, where: halo_copy(1, chunk, k, where).start(), ks)

    loads[8].wait()

    left8 = left_half[0:8]
    row8 = lax.broadcasted_iota(jnp.int32, (8, E), 0)

    def pack(q, carry):
        for p in range(Q):
            both = jnp.concatenate([solver[0, q, p], solver[1, q, p]], axis=0)
            turned = swap(both)
            fine_weights[q, p, 0:8, :] = jnp.where(left8, both, pltpu.roll(turned, 7, 0))
            fine_weights[q, p, 8:16, :] = jnp.where(left8, turned, pltpu.roll(both, 7, 0))
            ways = jnp.concatenate([star[q, p], jnp.zeros((5, E), f32)], axis=0)
            other = jnp.where(row8 == 0, pltpu.roll(swap(ways), 7, 0), 0.0)
            fine_weights[q, p, 16:24, :] = jnp.where(left8, ways, other)
        return carry

    lax.fori_loop(0, Q, pack, 0)
    gain_fine = twice(gain)

    loads[9].wait()
    for c in range(3):
        matrix_u[c * BP : (c + 1) * BP, :] = jnp.transpose(stiff[c])[0:BP]
    for f in range(4):
        stiff[3 + f, 0:B, 0:B] = wide_local[:, f, :]
        matrix_u[(3 + f) * BP : (4 + f) * BP, :] = -stiff[3 + f, 0:BP, :]

    def own_fine():
        put_stack(lambda p: twice(first[p]), 48)
        product = stacked_dot(make_stack(matrix_u[...], 48), 48)
        for p in range(Q):
            pieces = [product[g * BP : (g + 1) * BP, p * E : (p + 1) * E] for g in range(7)]
            applied[0, p] = jnp.where(left_half, pieces[0], pieces[1])
            applied[1, p] = pieces[2]
            applied[2, p] = jnp.where(left_half, pieces[3], pieces[4])
            applied[3, p] = jnp.where(left_half, pieces[5], pieces[6])

    def paired(ref):
        rows = [ref[f : f + 1, :] for f in range(4)]
        return [
            jnp.where(left_row, rows[0], swap(rows[1])),
            jnp.where(left_row, rows[2], swap(rows[3])),
            jnp.where(left_row, swap(rows[0]), rows[1]),
            jnp.where(left_row, swap(rows[2]), rows[3]),
        ]

    loads[12].wait()
    place = lax.broadcasted_iota(jnp.int32, (E, E), 0)

    def one_hot(mask):
        return jnp.where(mask, 1.0, 0.0).astype(bf16)

    sources = paired(source)

    def point():
        for k in range(4):
            right = jnp.concatenate([one_hot(place == row - (E + k * E)) for row in sources], axis=1)
            row = ROW_OF_SLOT[k]
            left = one_hot(place == side_got[k, row : row + 1, :])
            right = jnp.dot(left, right, preferred_element_type=f32).astype(bf16)
            pick[k, 0:E, :] = right
            pick[k, E : 2 * E, :] = right

    from_all(lambda k, where: side_copy(k, where).wait_recv())
    point()
    row = min_finish(0)
    min_start(1, row)

    loads[11].wait()
    selects = paired(select)
    loads[10].wait()
    flat[...] = jnp.zeros((B * BP, E), f32)
    for i in range(B):
        flat[pl.ds(i, B, stride=BP), 0:NSEL] = wide_flat[i]
    number = lax.rem(lax.broadcasted_iota(jnp.int32, (E, E), 0), NSEL)
    usable = lax.broadcasted_iota(jnp.int32, (E, E), 0) < 2 * NSEL
    hot = jnp.concatenate(
        [
            jnp.where(jnp.logical_and(number == row, usable), -1.0, 0.0).astype(bf16)
            for row in selects
        ],
        axis=1,
    )

    def choose(index, carry):
        rows = pl.ds(pl.multiple_of(index * 200, 8), 200)
        high, low = split(flat[rows, :])
        left = (high.astype(f32) + pltpu.roll(low.astype(f32), NSEL, 1)).astype(bf16)
        product = jnp.dot(left, hot, preferred_element_type=f32)
        for g in range(4):
            chosen[g, rows, :] = product[:, g * E : (g + 1) * E]
        return carry

    lax.fori_loop(0, 7, choose, 0)

    def gather(blocks):
        total = None
        for k in range(4):
            high, low = split(blocks[k])
            left = jnp.concatenate([high, low], axis=1)
            value = jnp.dot(left, pick[k], preferred_element_type=f32)
            total = value if total is None else total + value
        return total

    def gather_series(piece):
        height = HEIGHT[piece]
        for part_of in range(3):
            rows = slice(part_of * 3, part_of * 3 + 3)
            total = gather(
                [got[k, rows, START[piece] : START[piece] + height].reshape(3 * height, E) for k in range(4)]
            )
            for g in range(4):
                where = slice(part_of * 3 * height, (part_of + 1) * 3 * height)
                gathered[piece][g, where, :] = total[:, g * E : (g + 1) * E]

    def near(source_row, first_j, count, g, ps, sums):
        for j in range(count):
            matrix = chosen[g, (first_j + j) * BP : (first_j + j + 1) * BP, :]
            for n, p in enumerate(ps):
                sums[n] = sums[n] + matrix * source_row(p, j)
        return sums

    for chunk in range(CHUNKS):
        from_all(lambda k, where: halo_copy(0, chunk, k, where).wait_recv())

    gather_series(0)

    def face_before(g, carry):
        sums = [jnp.zeros((BP, E), f32) for _ in range(Q)]
        sums = near(lambda p, j: gathered_0[g, p * 32 + j : p * 32 + j + 1, :], 0, 32, g, range(Q), sums)
        for p in range(Q):
            face_terms[g, p] = sums[p]
        return carry

    lax.fori_loop(0, 2, face_before, 0)

    step = jnp.min(min_finish(1), axis=1, keepdims=True) * COURANT
    step = jnp.broadcast_to(step, (1, E))
    powers, value = [], 1.0
    for power in range(5):
        value = value * step / (power + 1)
        powers.append(value)
    late = [powers[k] * (2.0 ** (k + 1) - 1.0) for k in range(5)]

    def taylor(base, q, weight):
        whole = weight[0] * base[q]
        low = whole[0:8] + weight[1] * series_1[q, 0:8] + weight[2] * series_2[q, 0:8]
        low = low + weight[3] * series_3[q] + weight[4] * series_4[q]
        mid = whole[8:16] + weight[1] * series_1[q, 8:16] + weight[2] * series_2[q, 8:16]
        top = whole[16:24] + weight[1] * series_1[q, 16:24]
        return jnp.concatenate([low, mid, top, whole[24:BP]], axis=0)

    fine = coarse < 0.5
    for q in range(Q):
        first[q] = taylor(dof, q, powers)
        second[q] = taylor(dof, q, late)
    own_fine()
    changes = contract(fine_weight(0), range(4), BP, nothing(BP))
    for q in range(Q):
        part[0, q] = changes[q]

    def series_tiles(g, p):
        mixed = gathered_1[g, p * 40 : p * 40 + 8, :]
        high = [gathered_1[g, p * 40 + 8 * t : p * 40 + 8 * t + 8, :] for t in range(1, 5)]
        turned = pltpu.roll(high[3], 4, 0)
        d_1 = (high[0], high[1], jnp.where(sub8 < 4, high[2], 0.0))
        d_2 = (
            jnp.where(sub8 < 4, pltpu.roll(high[2], 4, 0), turned),
            jnp.where(sub8 < 2, turned, 0.0),
        )
        d_3 = jnp.where(sub8 < 4, pltpu.roll(mixed, 5, 0), 0.0)
        d_4 = jnp.where(sub8 < 1, pltpu.roll(mixed, 1, 0), 0.0)
        return mixed, d_1, d_2, d_3, d_4

    def summed_tiles(tiles, weight):
        mixed, d_1, d_2, d_3, d_4 = tiles
        return (
            weight[1] * d_1[0] + weight[2] * d_2[0] + weight[3] * d_3 + weight[4] * d_4,
            weight[1] * d_1[1] + weight[2] * d_2[1],
            weight[1] * d_1[2],
            weight[0] * mixed,
        )

    for chunk in range(CHUNKS):
        ps = range(chunk * PER, (chunk + 1) * PER)
        from_all(lambda k, where: halo_copy(1, chunk, k, where).wait_recv())
        gather_series(1)
        for g in range(2):
            for p in ps:
                for t, tile in enumerate(summed_tiles(series_tiles(g, p), powers)):
                    remote[g, p * BP + 8 * t : p * BP + 8 * t + 8, :] = tile

        def face_after(g, carry, ps=ps):
            sums = [powers[0] * face_terms[g, p] for p in ps]
            sums = near(lambda p, j: remote[g, p * BP + j : p * BP + j + 1, :], 0, 20, g, ps, sums)
            sums = near(lambda p, j: remote[g, p * BP + 24 + j : p * BP + 25 + j, :], 32, 3, g, ps, sums)
            for n, p in enumerate(ps):
                applied[4 + g, p] = sums[n]
            return carry

        lax.fori_loop(0, 2, face_after, 0)
    changes = contract(fine_weight(0), range(4, 6), BP, [part[0, q] for q in range(Q)])
    for q in range(Q):
        change = changes[q] + swap(changes[q])
        middle[q] = twice(dof[q]) + scaled(q, change, gain_fine)
    for index in range(4):
        base = middle if index == 0 else series[index]
        derive(lambda p, base=base: base[p], index, series[index + 1], True)
    fine_left = jnp.logical_and(fine, left_row)
    for q in range(Q):
        applied[10, q] = taylor(middle, q, powers)
        second[q] = jnp.where(fine_left, applied[10, q], second[q])

    energy = jnp.zeros((1, E), f32)
    for q in range(6):
        mean = (first[q, 0:1, :] + second[q, 0:1, :]) / (2.0 * step)
        energy = energy + mean * mean
    loads[13].wait()
    exposure = 2.0 * step * rate[...] * energy / (1.0 + energy)
    new_gain = gain * jnp.exp(-exposure)
    min_start(2, size[...] / (speed[...] * jnp.sqrt(new_gain)))
    damage_out[...] = 1.0 - new_gain

    fine_both = twice(jnp.where(fine, 1.0, 0.0))
    for n in range(5):
        other = applied[10, 2 * n + 1] if n < 4 else jnp.zeros((BP, E), f32)
        sent_b[n] = jnp.where(left_half, applied[10, 2 * n], other) * fine_both
    for chunk in range(CHUNKS):
        to_all(lambda k, where: halo_copy(2, chunk, k, where).start())

    put_stack(lambda p: second[p] + coarse * first[p], 48)
    product = stacked_dot(make_stack(matrix_u[...], 48), 48)
    for g in range(7):
        for p in range(Q):
            applied[g, p] = product[g * BP : (g + 1) * BP, p * E : (p + 1) * E]

    def own_weight(q, p, g):
        return star[q, p, g : g + 1, :] if g < 3 else solver[0, q, p, g - 3 : g - 2, :]

    sums = contract(own_weight, range(7), BP, nothing(BP))
    for q in range(Q):
        part[0, q] = sums[q]
    for q in range(Q):
        base = jnp.where(fine_left, middle[q], dof[q])
        middle[q] = base

    row = min_finish(2)
    min_start(3, row)

    coarse_halves = [
        jnp.where(left_row, coarse, swap(coarse)),
        jnp.where(left_row, swap(coarse), coarse),
    ]
    for g in range(4):
        theirs = gathered_1[g, MARK : MARK + 1, :]
        weight = [late[k] * theirs + powers[k] * coarse_halves[g // 2] for k in range(5)]
        for p in range(Q):
            tiles = summed_tiles(series_tiles(g, p), weight)
            value = [weight[0] * gathered_0[g, p * 32 + 8 * t : p * 32 + 8 * t + 8, :] for t in range(4)]
            value = [value[0] + tiles[0], value[1] + tiles[1], value[2] + tiles[2], value[3], tiles[3]]
            for t in range(5):
                remote[g, p * BP + 8 * t : p * BP + 8 * t + 8, :] = value[t]

    for k in range(4):
        pick[k, HALF:E, :] = jnp.zeros((HALF, 4 * E), bf16)
        pick[k, E + HALF : 2 * E, :] = jnp.zeros((HALF, 4 * E), bf16)

    for chunk, (start, stop) in enumerate(LAST):
        from_all(lambda k, where: halo_copy(2, chunk, k, where).wait_recv())
        ps = range(2 * start, min(2 * stop, Q))
        for n in range(start, stop):
            blocks = [got_b[k, n] for k in range(4)]
            total = gather([jnp.concatenate([x, swap(x)], axis=0) for x in blocks])
            for half in range(2 if n < 4 else 1):
                rows = slice((2 * n + half) * BP, (2 * n + half + 1) * BP)
                for g in range(4):
                    value = total[half * BP : (half + 1) * BP, g * E : (g + 1) * E]
                    remote[g, rows, :] = remote[g, rows, :] + value

        def last_face(g, carry, ps=ps):
            sums = [jnp.zeros((BP, E), f32) for _ in ps]
            sums = near(lambda p, j: remote[g, p * BP + j : p * BP + j + 1, :], 0, B, g, ps, sums)
            for n, p in enumerate(ps):
                applied[g, p] = sums[n]
            return carry

        lax.fori_loop(0, 4, last_face, 0)
    left_sums = contract(fine_weight(4), range(2), BP, nothing(BP))
    for q in range(Q):
        total = left_sums[q]
        part[1, q] = total + swap(total)
    right_sums = contract(fine_weight(4), range(2, 4), BP, nothing(BP))
    for q in range(Q):
        total = right_sums[q]
        value = part[0, q] + jnp.where(left_half, part[1, q], total + swap(total))
        dof_out[q] = (middle[q] + scaled(q, value, gain))[0:B]

    step_out[...] = COURANT * jnp.min(min_finish(3), axis=1, keepdims=True)

    for stage in range(4):
        min_drain(stage)

    def drain(k, where):
        side_copy(k, where).wait_send()
        for piece in range(3):
            for chunk in range(CHUNKS):
                halo_copy(piece, chunk, k, where).wait_send()

    to_all(drain)


def shards(
    n_strike,
    n_depth,
    dof_values,
    star_matrices,
    flux_solvers,
    stiffness,
    flux_local,
    flux_neighbour,
    flux_select,
    face_source,
    side_list,
    cluster_ids,
    damage,
    element_size,
    wave_speed,
    damage_rate,
):
    out_shape = (
        jax.ShapeDtypeStruct((Q, B, E), f32),
        jax.ShapeDtypeStruct((1, E), f32),
        jax.ShapeDtypeStruct((1, 1), f32),
    )
    most = max(n_strike, n_depth)
    vmem = pltpu.VMEM
    dma = pltpu.SemaphoreType.DMA
    call = pl.pallas_call(
        functools.partial(kernel, n_strike, n_depth),
        out_shape=out_shape,
        in_specs=[pl.BlockSpec(memory_space=pltpu.HBM)] * 14,
        out_specs=tuple(pl.BlockSpec(memory_space=pltpu.VMEM) for _ in range(3)),
        scratch_shapes=[
            vmem((Q, B, E), f32),
            vmem((Q, Q, 3, E), f32),
            vmem((2, Q, Q, 4, E), f32),
            vmem((3, B, B), f32),
            vmem((B, 4, B), f32),
            vmem((B, B, NSEL), f32),
            vmem((4, E), jnp.int32),
            vmem((4, E), jnp.int32),
            vmem((4, E), jnp.int32),
            vmem((1, E), jnp.int32),
            vmem((1, E), f32),
            vmem((1, E), f32),
            vmem((1, E), f32),
            vmem((1, E), f32),
            vmem((4, most, 1, E), f32),
            vmem((4, 4, E), jnp.int32),
            vmem((Q, BP, E), f32),
            vmem((Q, SENT, E), f32),
            vmem((5, BP, E), f32),
            vmem((4, Q, SENT, E), f32),
            vmem((4, 5, BP, E), f32),
            vmem((Q, 24, E), f32),
            vmem((Q, 16, E), f32),
            vmem((Q, 8, E), f32),
            vmem((Q, 8, E), f32),
            vmem((Q, BP, E), f32),
            vmem((Q, BP, E), f32),
            vmem((Q, BP, E), f32),
            vmem((7, E, E), f32),
            vmem((B * BP, E), f32),
            vmem((Q, Q, 24, E), f32),
            vmem((256, Q * E), bf16),
            vmem((72, E), f32),
            vmem((48, E), f32),
            vmem((24, E), f32),
            vmem((280, E), f32),
            vmem((11, Q, BP, E), f32),
            vmem((2, Q, BP, E), f32),
            vmem((2, Q, BP, E), f32),
            vmem((4, B * BP, E), f32),
            vmem((4, 2 * E, 4 * E), bf16),
            vmem((4, Q * HEIGHT[0], E), f32),
            vmem((4, Q * HEIGHT[1], E), f32),
            vmem((4, Q * BP, E), f32),
            dma((14,)),
            dma((4, most)),
            dma((4, most)),
            dma((4,)),
            dma((4,)),
            dma((3, CHUNKS, 4)),
            dma((3, CHUNKS, 4)),
        ],
        compiler_params=pltpu.CompilerParams(
            collective_id=0, has_side_effects=True, vmem_limit_bytes=32 * 1024 * 1024
        ),
    )
    row = (1, E)
    operands = (
        dof_values,
        jnp.transpose(star_matrices, (1, 2, 0, 3)),
        jnp.transpose(flux_solvers, (0, 2, 3, 1, 4)),
        stiffness,
        jnp.transpose(flux_local, (1, 0, 2)),
        jnp.transpose(flux_neighbour, (1, 2, 0)),
        flux_select,
        face_source,
        side_list,
        cluster_ids.reshape(row),
        damage.reshape(row),
        element_size.reshape(row),
        wave_speed.reshape(row),
        damage_rate.reshape(row),
    )
    final, new_damage, next_step = call(
        *(pltpu.with_memory_space_constraint(x, pltpu.HBM) for x in operands)
    )
    return final, new_damage.reshape(E), next_step.reshape(())


def solution(mesh):
    both = ("strike", "depth")
    in_specs = (
        P(None, None, both),
        P(None, None, None, both),
        P(None, None, None, None, both),
        P(),
        P(),
        P(),
        P(None, both),
        P(None, both),
        P(None, both),
        P(both),
        P(both),
        P(both),
        P(both),
        P(both),
    )
    out_specs = (P(None, None, both), P(both), P())
    body = functools.partial(shards, mesh.shape["strike"], mesh.shape["depth"])
    return jax.shard_map(body, mesh=mesh, in_specs=in_specs, out_specs=out_specs, check_vma=False)
```

```python
import functools

import jax
import jax.numpy as jnp
from jax import lax
from jax.experimental import pallas as pl
from jax.experimental.pallas import tpu as pltpu
from jax.sharding import PartitionSpec as P

COURANT = 1.0
Q = 9
B = 35
BP = 40
E = 128
HALF = 64
NSEL = 48
MESH = pl.DeviceIdType.MESH
f32, bf16 = jnp.float32, jnp.bfloat16
ROW_OF_SLOT = (1, 0, 3, 2)
START, HEIGHT = (0, 32), (32, 40)
SENT = 72
MARK = 38
CHUNKS = 1
PER = Q // CHUNKS
STAGES = ("strike", "depth", "depth", "strike")
LAST = ((0, 5),)
ROWS = (40, 24, 16, 8, 8)
SLOTS = (48, 32, 16, 16, 16)


def split(x):
    high = x.astype(bf16)
    return high, (x - high.astype(f32)).astype(bf16)


def third_of(slot):
    return 2 * slot if 3 * slot <= 128 else 128


def make_stack(matrix, slot):
    lane = lax.broadcasted_iota(jnp.int32, matrix.shape, 1)
    high, low = split(jnp.where(lane < slot, matrix, 0.0))
    high, low = high.astype(f32), low.astype(f32)
    if 3 * slot <= 128:
        return (high + pltpu.roll(high, slot, 1) + pltpu.roll(low, 2 * slot, 1)).astype(bf16)
    return jnp.concatenate([high + pltpu.roll(high, slot, 1), low], axis=1).astype(bf16)


def degree_of(index):
    degree = jnp.zeros_like(index)
    for first in (1, 4, 10, 20):
        degree = degree + jnp.where(index >= first, 1, 0)
    return degree


def kernel(
    n_strike,
    n_depth,
    dof_in,
    star_in,
    solver_in,
    stiff_in,
    local_in,
    flat_in,
    select_in,
    source_in,
    side_in,
    cluster_in,
    damage_in,
    size_in,
    speed_in,
    rate_in,
    dof_out,
    damage_out,
    step_out,
    dof_raw,
    star,
    solver,
    wide_stiff,
    wide_local,
    wide_flat,
    select,
    source,
    side,
    cluster,
    damage,
    size,
    speed,
    rate,
    mine,
    minima,
    side_got,
    dof,
    sent,
    sent_b,
    got,
    got_b,
    series_1,
    series_2,
    series_3,
    series_4,
    first,
    second,
    middle,
    stiff,
    flat,
    fine_weights,
    stack,
    matrix_0,
    matrix_1,
    matrix_2,
    matrix_u,
    applied,
    face_terms,
    part,
    chosen,
    pick,
    gathered_0,
    gathered_1,
    remote,
    load_sem,
    min_send,
    min_recv,
    side_send,
    side_recv,
    halo_send,
    halo_recv,
):
    s, d = lax.axis_index("strike"), lax.axis_index("depth")
    gathered = (gathered_0, gathered_1)
    series = (dof, series_1, series_2, series_3, series_4)

    loads = [
        pltpu.make_async_copy(src, dst, load_sem.at[index])
        for index, (src, dst) in enumerate(
            [
                (damage_in, damage),
                (size_in, size),
                (speed_in, speed),
                (dof_in, dof_raw),
                (side_in, side),
                (stiff_in, wide_stiff),
                (star_in, star),
                (cluster_in, cluster),
                (solver_in, solver),
                (local_in, wide_local),
                (flat_in, wide_flat),
                (select_in, select),
                (source_in, source),
                (rate_in, rate),
            ]
        )
    ]

    for load in loads[0:3]:
        load.start()

    barrier = pltpu.get_barrier_semaphore()
    groups = {"depth": (d, n_depth), "strike": (s, n_strike)}
    order = sorted(range(1, max(n_depth, n_strike)), key=lambda off: abs(off - n_depth / 2))
    for off in order:
        for axis, (me, count) in groups.items():
            if off < count:
                pl.semaphore_signal(
                    barrier, inc=1, device_id={axis: lax.rem(me + off, count)}, device_id_type=MESH
                )
    for load in loads[3:]:
        load.start()

    has = (s > 0, s < n_strike - 1, d > 0, d < n_depth - 1)
    towards = (
        (s < n_strike - 1, {"strike": lax.rem(s + 1, n_strike)}),
        (s > 0, {"strike": lax.rem(s + n_strike - 1, n_strike)}),
        (d < n_depth - 1, {"depth": lax.rem(d + 1, n_depth)}),
        (d > 0, {"depth": lax.rem(d + n_depth - 1, n_depth)}),
    )

    def min_copy(stage, off):
        axis = STAGES[stage]
        me, count = groups[axis]
        return pltpu.make_async_remote_copy(
            src_ref=mine.at[stage],
            dst_ref=minima.at[stage, off - 1],
            send_sem=min_send.at[stage, off],
            recv_sem=min_recv.at[stage],
            device_id={axis: lax.rem(me + off, count)},
            device_id_type=MESH,
        )

    def min_offsets(stage):
        return [off for off in order if off < groups[STAGES[stage]][1]]

    def min_start(stage, row):
        mine[stage] = row
        for off in min_offsets(stage):
            min_copy(stage, off).start()

    def min_finish(stage):
        axis = STAGES[stage]
        me, count = groups[axis]
        rows = [mine[stage]]
        if count > 1:
            others = minima.at[stage, pl.ds(0, count - 1)]
            pltpu.make_async_remote_copy(
                src_ref=others,
                dst_ref=others,
                send_sem=min_send.at[stage, 0],
                recv_sem=min_recv.at[stage],
                device_id={axis: lax.rem(me + 1, count)},
                device_id_type=MESH,
            ).wait_recv()
            rows += [minima[stage, other] for other in range(count - 1)]
        while len(rows) > 1:
            rows = [jnp.minimum(a, b) for a, b in zip(rows[::2], rows[1::2])] + rows[len(rows) // 2 * 2 :]
        return rows[0]

    def min_drain(stage):
        for off in min_offsets(stage):
            min_copy(stage, off).wait_send()

    def halo_copy(piece, chunk, k, where):
        if piece < 2:
            rows = pl.ds(chunk * PER, PER)
            height = pl.ds(START[piece], HEIGHT[piece])
            src, dst = sent.at[rows, height], got.at[k, rows, height]
        else:
            rows = pl.ds(LAST[chunk][0], LAST[chunk][1] - LAST[chunk][0])
            src, dst = sent_b.at[rows], got_b.at[k, rows]
        return pltpu.make_async_remote_copy(
            src_ref=src,
            dst_ref=dst,
            send_sem=halo_send.at[piece, chunk, k],
            recv_sem=halo_recv.at[piece, chunk, k],
            device_id=where,
            device_id_type=MESH,
        )

    def side_copy(k, where):
        return pltpu.make_async_remote_copy(
            src_ref=side,
            dst_ref=side_got.at[k],
            send_sem=side_send.at[k],
            recv_sem=side_recv.at[k],
            device_id=where,
            device_id_type=MESH,
        )

    def to_all(send, ks=range(4)):
        for k in ks:
            exists, where = towards[k]

            @pl.when(exists)
            def _(k=k, where=where):
                send(k, where)

    def from_all(receive):
        for k in range(4):

            @pl.when(has[k])
            def _(k=k):
                receive(k, towards[k][1])

    left_half = lax.broadcasted_iota(jnp.int32, (BP, E), 1) < HALF
    left_row = left_half[0:1]
    sub = lax.broadcasted_iota(jnp.int32, (BP, E), 0)
    lane = lax.broadcasted_iota(jnp.int32, (BP, E), 1)

    def swap(x):
        return pltpu.roll(x, HALF, 1)

    def twice(x):
        return jnp.where(left_half[0 : x.shape[0]], x, swap(x))

    for load in loads[0:3]:
        load.wait()
    gain = 1.0 - damage[...]
    own_ratio = size[...] / (speed[...] * jnp.sqrt(gain))
    pl.semaphore_wait(barrier, n_depth + n_strike - 2)
    min_start(0, own_ratio)
    loads[3].wait()
    for q in range(Q):
        sent[q, 0:32, :] = dof_raw[q, 0:32, :]
    for ks in ((0, 1), (2, 3)):
        for chunk in range(CHUNKS):
            to_all(lambda k, where: halo_copy(0, chunk, k, where).start(), ks)
    loads[4].wait()
    to_all(lambda k, where: side_copy(k, where).start())

    for k in range(4):

        @pl.when(jnp.logical_not(has[k]))
        def _(k=k):
            got[k] = jnp.zeros((Q, SENT, E), f32)
            got_b[k] = jnp.zeros((5, BP, E), f32)
            side_got[k] = jnp.full((4, E), -1, jnp.int32)

    stack[96:128, :] = jnp.zeros((32, Q * E), bf16)
    stack[176:256, :] = jnp.zeros((80, Q * E), bf16)
    stiff[...] = jnp.zeros((7, E, E), f32)

    loads[7].wait()
    coarse = jnp.where(cluster[...] != 0, 1.0, 0.0)
    for q in range(Q):
        dof[q, 32:BP, :] = jnp.zeros((8, E), f32)
        dof[q, 0:B, :] = dof_raw[q]

    loads[5].wait()
    inside = jnp.logical_and(sub < B, lane < B)
    keep = jnp.logical_and(inside, degree_of(sub) < degree_of(lane))
    for c in range(3):
        stiff[c, 0:B, 0:B] = wide_stiff[c]
        kept = jnp.where(keep, stiff[c, 0:BP, :], 0.0)
        stiff[c, 0:BP, :] = kept
        matrix_0[c * 24 : (c + 1) * 24, :] = kept[0:24]
        matrix_1[c * 16 : (c + 1) * 16, :] = jnp.where(lane[0:16] < 20, kept[0:16], 0.0)
        matrix_2[c * 8 : (c + 1) * 8, :] = jnp.where(lane[0:8] < 10, kept[0:8], 0.0)

    def put_stack(source_rows, slot):
        third = third_of(slot)
        for p in range(Q):
            x = source_rows(p)
            if x.shape[0] < slot:
                x = jnp.concatenate([x, jnp.zeros((slot - x.shape[0], E), f32)], axis=0)
            high, low = split(x)
            columns = pl.ds(p * E, E)
            stack[0:slot, columns] = high
            stack[slot : 2 * slot, columns] = low
            stack[third : third + slot, columns] = high

    def stacked_dot(left, slot):
        rows = 256 if 3 * slot > 128 else 3 * slot
        return jnp.dot(left[:, 0:rows], stack[0:rows, :], preferred_element_type=f32)

    def contract(weight, pieces, rows, sums):
        def body(p, sums):
            sums = list(sums)
            for g in pieces:
                field = applied[g, p, 0:rows, :]
                for q in range(Q):
                    sums[q] = sums[q] + weight(q, p, g) * field
            return tuple(sums)

        if rows <= 24:
            for p in range(Q):
                sums = body(p, sums)
            return sums
        return lax.fori_loop(0, Q, body, tuple(sums))

    def nothing(rows):
        return [jnp.zeros((rows, E), f32) for _ in range(Q)]

    def scaled(q, x, by):
        return x * by if q < 6 else x

    def star_weight(q, p, c):
        return star[q, p, c : c + 1, :]

    pack_rows = (16, 18, 0, 2, 4, 6, 12, 14)

    def fine_weight(shift):
        def weight(q, p, g):
            row = pack_rows[g + shift]
            return fine_weights[q, p, row : row + 1, :]

        return weight

    def derive(source_rows, order_in, target, fine):
        matrix = (matrix_0, matrix_1, matrix_2, matrix_2)[order_in]
        rows, slot = (24, 16, 8, 8)[order_in], SLOTS[order_in]
        put_stack(source_rows, slot)
        product = stacked_dot(make_stack(matrix[...], slot), slot)
        for p in range(Q):
            pieces = [product[c * rows : (c + 1) * rows, p * E : (p + 1) * E] for c in range(3)]
            if fine:
                pieces = [jnp.where(left_half[0:rows], pieces[0], pieces[1]), pieces[2]]
            for g, piece in enumerate(pieces):
                applied[g, p, 0:rows, :] = piece
        if fine:
            sums = contract(fine_weight(0), range(2), rows, nothing(rows))
        else:
            sums = contract(star_weight, range(3), rows, nothing(rows))
        for q in range(Q):
            total = sums[q] + swap(sums[q]) if fine else sums[q]
            target[q] = -scaled(q, total, gain_fine if fine else gain)

    loads[6].wait()
    for index in range(4):
        derive(lambda p, index=index: series[index][p], index, series[index + 1], False)
    sub8 = lax.broadcasted_iota(jnp.int32, (8, E), 0)
    for q in range(Q):
        turned = pltpu.roll(series_2[q, 0:8], 4, 0)
        sent[q, 32:40, :] = (
            dof[q, 32:BP, :] + pltpu.roll(series_3[q], 3, 0) + pltpu.roll(series_4[q], 7, 0)
        )
        sent[q, 40:56, :] = series_1[q, 0:16]
        sent[q, 56:64, :] = series_1[q, 16:24] + jnp.where(sub8 >= 4, turned, 0.0)
        sent[q, 64:72, :] = jnp.where(sub8 < 4, turned, 0.0) + pltpu.roll(series_2[q, 8:16], 4, 0)
    sent[0, 32 + MARK : 33 + MARK, :] = coarse
    for ks in ((0, 1), (2, 3)):
        for chunk in range(CHUNKS):
            to_all(lambda k, where: halo_copy(1, chunk, k, where).start(), ks)

    loads[8].wait()

    left8 = left_half[0:8]
    row8 = lax.broadcasted_iota(jnp.int32, (8, E), 0)

    def pack(q, carry):
        for p in range(Q):
            both = jnp.concatenate([solver[0, q, p], solver[1, q, p]], axis=0)
            turned = swap(both)
            fine_weights[q, p, 0:8, :] = jnp.where(left8, both, pltpu.roll(turned, 7, 0))
            fine_weights[q, p, 8:16, :] = jnp.where(left8, turned, pltpu.roll(both, 7, 0))
            ways = jnp.concatenate([star[q, p], jnp.zeros((5, E), f32)], axis=0)
            other = jnp.where(row8 == 0, pltpu.roll(swap(ways), 7, 0), 0.0)
            fine_weights[q, p, 16:24, :] = jnp.where(left8, ways, other)
        return carry

    lax.fori_loop(0, Q, pack, 0)
    gain_fine = twice(gain)

    loads[9].wait()
    for c in range(3):
        matrix_u[c * BP : (c + 1) * BP, :] = jnp.transpose(stiff[c])[0:BP]
    for f in range(4):
        stiff[3 + f, 0:B, 0:B] = wide_local[:, f, :]
        matrix_u[(3 + f) * BP : (4 + f) * BP, :] = -stiff[3 + f, 0:BP, :]

    def own_fine():
        put_stack(lambda p: twice(first[p]), 48)
        product = stacked_dot(make_stack(matrix_u[...], 48), 48)
        for p in range(Q):
            pieces = [product[g * BP : (g + 1) * BP, p * E : (p + 1) * E] for g in range(7)]
            applied[0, p] = jnp.where(left_half, pieces[0], pieces[1])
            applied[1, p] = pieces[2]
            applied[2, p] = jnp.where(left_half, pieces[3], pieces[4])
            applied[3, p] = jnp.where(left_half, pieces[5], pieces[6])

    def paired(ref):
        rows = [ref[f : f + 1, :] for f in range(4)]
        return [
            jnp.where(left_row, rows[0], swap(rows[1])),
            jnp.where(left_row, rows[2], swap(rows[3])),
            jnp.where(left_row, swap(rows[0]), rows[1]),
            jnp.where(left_row, swap(rows[2]), rows[3]),
        ]

    loads[12].wait()
    place = lax.broadcasted_iota(jnp.int32, (E, E), 0)

    def one_hot(mask):
        return jnp.where(mask, 1.0, 0.0).astype(bf16)

    sources = paired(source)

    def point():
        for k in range(4):
            right = jnp.concatenate([one_hot(place == row - (E + k * E)) for row in sources], axis=1)
            row = ROW_OF_SLOT[k]
            left = one_hot(place == side_got[k, row : row + 1, :])
            right = jnp.dot(left, right, preferred_element_type=f32).astype(bf16)
            pick[k, 0:E, :] = right
            pick[k, E : 2 * E, :] = right

    from_all(lambda k, where: side_copy(k, where).wait_recv())
    point()
    row = min_finish(0)
    min_start(1, row)

    loads[11].wait()
    selects = paired(select)
    loads[10].wait()
    flat[...] = jnp.zeros((B * BP, E), f32)
    for i in range(B):
        flat[pl.ds(i, B, stride=BP), 0:NSEL] = wide_flat[i]
    number = lax.rem(lax.broadcasted_iota(jnp.int32, (E, E), 0), NSEL)
    usable = lax.broadcasted_iota(jnp.int32, (E, E), 0) < 2 * NSEL
    hot = jnp.concatenate(
        [
            jnp.where(jnp.logical_and(number == row, usable), -1.0, 0.0).astype(bf16)
            for row in selects
        ],
        axis=1,
    )

    def choose(index, carry):
        rows = pl.ds(pl.multiple_of(index * 200, 8), 200)
        high, low = split(flat[rows, :])
        left = (high.astype(f32) + pltpu.roll(low.astype(f32), NSEL, 1)).astype(bf16)
        product = jnp.dot(left, hot, preferred_element_type=f32)
        for g in range(4):
            chosen[g, rows, :] = product[:, g * E : (g + 1) * E]
        return carry

    lax.fori_loop(0, 7, choose, 0)

    def gather(blocks):
        total = None
        for k in range(4):
            high, low = split(blocks[k])
            left = jnp.concatenate([high, low], axis=1)
            value = jnp.dot(left, pick[k], preferred_element_type=f32)
            total = value if total is None else total + value
        return total

    def gather_series(piece):
        height = HEIGHT[piece]
        for part_of in range(3):
            rows = slice(part_of * 3, part_of * 3 + 3)
            total = gather(
                [got[k, rows, START[piece] : START[piece] + height].reshape(3 * height, E) for k in range(4)]
            )
            for g in range(4):
                where = slice(part_of * 3 * height, (part_of + 1) * 3 * height)
                gathered[piece][g, where, :] = total[:, g * E : (g + 1) * E]

    def near(source_row, first_j, count, g, ps, sums):
        for j in range(count):
            matrix = chosen[g, (first_j + j) * BP : (first_j + j + 1) * BP, :]
            for n, p in enumerate(ps):
                sums[n] = sums[n] + matrix * source_row(p, j)
        return sums

    for chunk in range(CHUNKS):
        from_all(lambda k, where: halo_copy(0, chunk, k, where).wait_recv())

    gather_series(0)

    def face_before(g, carry):
        sums = [jnp.zeros((BP, E), f32) for _ in range(Q)]
        sums = near(lambda p, j: gathered_0[g, p * 32 + j : p * 32 + j + 1, :], 0, 32, g, range(Q), sums)
        for p in range(Q):
            face_terms[g, p] = sums[p]
        return carry

    lax.fori_loop(0, 2, face_before, 0)

    step = jnp.min(min_finish(1), axis=1, keepdims=True) * COURANT
    step = jnp.broadcast_to(step, (1, E))
    powers, value = [], 1.0
    for power in range(5):
        value = value * step / (power + 1)
        powers.append(value)
    late = [powers[k] * (2.0 ** (k + 1) - 1.0) for k in range(5)]

    def taylor(base, q, weight):
        whole = weight[0] * base[q]
        low = whole[0:8] + weight[1] * series_1[q, 0:8] + weight[2] * series_2[q, 0:8]
        low = low + weight[3] * series_3[q] + weight[4] * series_4[q]
        mid = whole[8:16] + weight[1] * series_1[q, 8:16] + weight[2] * series_2[q, 8:16]
        top = whole[16:24] + weight[1] * series_1[q, 16:24]
        return jnp.concatenate([low, mid, top, whole[24:BP]], axis=0)

    fine = coarse < 0.5
    for q in range(Q):
        first[q] = taylor(dof, q, powers)
        second[q] = taylor(dof, q, late)
    own_fine()
    changes = contract(fine_weight(0), range(4), BP, nothing(BP))
    for q in range(Q):
        part[0, q] = changes[q]

    def series_tiles(g, p):
        mixed = gathered_1[g, p * 40 : p * 40 + 8, :]
        high = [gathered_1[g, p * 40 + 8 * t : p * 40 + 8 * t + 8, :] for t in range(1, 5)]
        turned = pltpu.roll(high[3], 4, 0)
        d_1 = (high[0], high[1], jnp.where(sub8 < 4, high[2], 0.0))
        d_2 = (
            jnp.where(sub8 < 4, pltpu.roll(high[2], 4, 0), turned),
            jnp.where(sub8 < 2, turned, 0.0),
        )
        d_3 = jnp.where(sub8 < 4, pltpu.roll(mixed, 5, 0), 0.0)
        d_4 = jnp.where(sub8 < 1, pltpu.roll(mixed, 1, 0), 0.0)
        return mixed, d_1, d_2, d_3, d_4

    def summed_tiles(tiles, weight):
        mixed, d_1, d_2, d_3, d_4 = tiles
        return (
            weight[1] * d_1[0] + weight[2] * d_2[0] + weight[3] * d_3 + weight[4] * d_4,
            weight[1] * d_1[1] + weight[2] * d_2[1],
            weight[1] * d_1[2],
            weight[0] * mixed,
        )

    for chunk in range(CHUNKS):
        ps = range(chunk * PER, (chunk + 1) * PER)
        from_all(lambda k, where: halo_copy(1, chunk, k, where).wait_recv())
        gather_series(1)
        for g in range(2):
            for p in ps:
                for t, tile in enumerate(summed_tiles(series_tiles(g, p), powers)):
                    remote[g, p * BP + 8 * t : p * BP + 8 * t + 8, :] = tile

        def face_after(g, carry, ps=ps):
            sums = [powers[0] * face_terms[g, p] for p in ps]
            sums = near(lambda p, j: remote[g, p * BP + j : p * BP + j + 1, :], 0, 20, g, ps, sums)
            sums = near(lambda p, j: remote[g, p * BP + 24 + j : p * BP + 25 + j, :], 32, 3, g, ps, sums)
            for n, p in enumerate(ps):
                applied[4 + g, p] = sums[n]
            return carry

        lax.fori_loop(0, 2, face_after, 0)
    changes = contract(fine_weight(0), range(4, 6), BP, [part[0, q] for q in range(Q)])
    for q in range(Q):
        change = changes[q] + swap(changes[q])
        middle[q] = twice(dof[q]) + scaled(q, change, gain_fine)
    for index in range(4):
        base = middle if index == 0 else series[index]
        derive(lambda p, base=base: base[p], index, series[index + 1], True)
    fine_left = jnp.logical_and(fine, left_row)
    for q in range(Q):
        applied[10, q] = taylor(middle, q, powers)
        second[q] = jnp.where(fine_left, applied[10, q], second[q])

    energy = jnp.zeros((1, E), f32)
    for q in range(6):
        mean = (first[q, 0:1, :] + second[q, 0:1, :]) / (2.0 * step)
        energy = energy + mean * mean
    loads[13].wait()
    exposure = 2.0 * step * rate[...] * energy / (1.0 + energy)
    new_gain = gain * jnp.exp(-exposure)
    min_start(2, size[...] / (speed[...] * jnp.sqrt(new_gain)))
    damage_out[...] = 1.0 - new_gain

    fine_both = twice(jnp.where(fine, 1.0, 0.0))
    for n in range(5):
        other = applied[10, 2 * n + 1] if n < 4 else jnp.zeros((BP, E), f32)
        sent_b[n] = jnp.where(left_half, applied[10, 2 * n], other) * fine_both
    for chunk in range(CHUNKS):
        to_all(lambda k, where: halo_copy(2, chunk, k, where).start())

    put_stack(lambda p: second[p] + coarse * first[p], 48)
    product = stacked_dot(make_stack(matrix_u[...], 48), 48)
    for g in range(7):
        for p in range(Q):
            applied[g, p] = product[g * BP : (g + 1) * BP, p * E : (p + 1) * E]

    def own_weight(q, p, g):
        return star[q, p, g : g + 1, :] if g < 3 else solver[0, q, p, g - 3 : g - 2, :]

    sums = contract(own_weight, range(7), BP, nothing(BP))
    for q in range(Q):
        part[0, q] = sums[q]
    for q in range(Q):
        base = jnp.where(fine_left, middle[q], dof[q])
        middle[q] = base


    coarse_halves = [
        jnp.where(left_row, coarse, swap(coarse)),
        jnp.where(left_row, swap(coarse), coarse),
    ]
    for g in range(4):
        theirs = gathered_1[g, MARK : MARK + 1, :]
        weight = [late[k] * theirs + powers[k] * coarse_halves[g // 2] for k in range(5)]
        for p in range(Q):
            tiles = summed_tiles(series_tiles(g, p), weight)
            value = [weight[0] * gathered_0[g, p * 32 + 8 * t : p * 32 + 8 * t + 8, :] for t in range(4)]
            value = [value[0] + tiles[0], value[1] + tiles[1], value[2] + tiles[2], value[3], tiles[3]]
            for t in range(5):
                remote[g, p * BP + 8 * t : p * BP + 8 * t + 8, :] = value[t]

    for k in range(4):
        pick[k, HALF:E, :] = jnp.zeros((HALF, 4 * E), bf16)
        pick[k, E + HALF : 2 * E, :] = jnp.zeros((HALF, 4 * E), bf16)

    for stage in range(2):
        min_drain(stage)
    to_all(lambda k, where: side_copy(k, where).wait_send())
    for piece in range(2):
        for chunk in range(CHUNKS):
            to_all(lambda k, where: halo_copy(piece, chunk, k, where).wait_send())

    row = min_finish(2)
    min_start(3, row)
    for chunk, (start, stop) in enumerate(LAST):
        from_all(lambda k, where: halo_copy(2, chunk, k, where).wait_recv())
        ps = range(2 * start, min(2 * stop, Q))
        for n in range(start, stop):
            blocks = [got_b[k, n] for k in range(4)]
            total = gather([jnp.concatenate([x, swap(x)], axis=0) for x in blocks])
            for half in range(2 if n < 4 else 1):
                rows = slice((2 * n + half) * BP, (2 * n + half + 1) * BP)
                for g in range(4):
                    value = total[half * BP : (half + 1) * BP, g * E : (g + 1) * E]
                    remote[g, rows, :] = remote[g, rows, :] + value

        def last_face(g, carry, ps=ps):
            sums = [jnp.zeros((BP, E), f32) for _ in ps]
            sums = near(lambda p, j: remote[g, p * BP + j : p * BP + j + 1, :], 0, B, g, ps, sums)
            for n, p in enumerate(ps):
                applied[g, p] = sums[n]
            return carry

        lax.fori_loop(0, 4, last_face, 0)
    left_sums = contract(fine_weight(4), range(2), BP, nothing(BP))
    for q in range(Q):
        total = left_sums[q]
        part[1, q] = total + swap(total)
    right_sums = contract(fine_weight(4), range(2, 4), BP, nothing(BP))
    for q in range(Q):
        total = right_sums[q]
        value = part[0, q] + jnp.where(left_half, part[1, q], total + swap(total))
        dof_out[q] = (middle[q] + scaled(q, value, gain))[0:B]

    min_drain(2)
    for chunk in range(CHUNKS):
        to_all(lambda k, where: halo_copy(2, chunk, k, where).wait_send())
    step_out[...] = COURANT * jnp.min(min_finish(3), axis=1, keepdims=True)
    min_drain(3)


def shards(
    n_strike,
    n_depth,
    dof_values,
    star_matrices,
    flux_solvers,
    stiffness,
    flux_local,
    flux_neighbour,
    flux_select,
    face_source,
    side_list,
    cluster_ids,
    damage,
    element_size,
    wave_speed,
    damage_rate,
):
    out_shape = (
        jax.ShapeDtypeStruct((Q, B, E), f32),
        jax.ShapeDtypeStruct((1, E), f32),
        jax.ShapeDtypeStruct((1, 1), f32),
    )
    most = max(n_strike, n_depth)
    vmem = pltpu.VMEM
    dma = pltpu.SemaphoreType.DMA
    call = pl.pallas_call(
        functools.partial(kernel, n_strike, n_depth),
        out_shape=out_shape,
        in_specs=[pl.BlockSpec(memory_space=pltpu.HBM)] * 14,
        out_specs=tuple(pl.BlockSpec(memory_space=pltpu.VMEM) for _ in range(3)),
        scratch_shapes=[
            vmem((Q, B, E), f32),
            vmem((Q, Q, 3, E), f32),
            vmem((2, Q, Q, 4, E), f32),
            vmem((3, B, B), f32),
            vmem((B, 4, B), f32),
            vmem((B, B, NSEL), f32),
            vmem((4, E), jnp.int32),
            vmem((4, E), jnp.int32),
            vmem((4, E), jnp.int32),
            vmem((1, E), jnp.int32),
            vmem((1, E), f32),
            vmem((1, E), f32),
            vmem((1, E), f32),
            vmem((1, E), f32),
            vmem((4, 1, E), f32),
            vmem((4, most - 1 if most > 1 else 1, 1, E), f32),
            vmem((4, 4, E), jnp.int32),
            vmem((Q, BP, E), f32),
            vmem((Q, SENT, E), f32),
            vmem((5, BP, E), f32),
            vmem((4, Q, SENT, E), f32),
            vmem((4, 5, BP, E), f32),
            vmem((Q, 24, E), f32),
            vmem((Q, 16, E), f32),
            vmem((Q, 8, E), f32),
            vmem((Q, 8, E), f32),
            vmem((Q, BP, E), f32),
            vmem((Q, BP, E), f32),
            vmem((Q, BP, E), f32),
            vmem((7, E, E), f32),
            vmem((B * BP, E), f32),
            vmem((Q, Q, 24, E), f32),
            vmem((256, Q * E), bf16),
            vmem((72, E), f32),
            vmem((48, E), f32),
            vmem((24, E), f32),
            vmem((280, E), f32),
            vmem((11, Q, BP, E), f32),
            vmem((2, Q, BP, E), f32),
            vmem((2, Q, BP, E), f32),
            vmem((4, B * BP, E), f32),
            vmem((4, 2 * E, 4 * E), bf16),
            vmem((4, Q * HEIGHT[0], E), f32),
            vmem((4, Q * HEIGHT[1], E), f32),
            vmem((4, Q * BP, E), f32),
            dma((14,)),
            dma((4, most)),
            dma((4,)),
            dma((4,)),
            dma((4,)),
            dma((3, CHUNKS, 4)),
            dma((3, CHUNKS, 4)),
        ],
        compiler_params=pltpu.CompilerParams(
            collective_id=0, has_side_effects=True, vmem_limit_bytes=32 * 1024 * 1024
        ),
    )
    row = (1, E)
    operands = (
        dof_values,
        jnp.transpose(star_matrices, (1, 2, 0, 3)),
        jnp.transpose(flux_solvers, (0, 2, 3, 1, 4)),
        stiffness,
        jnp.transpose(flux_local, (1, 0, 2)),
        jnp.transpose(flux_neighbour, (1, 2, 0)),
        flux_select,
        face_source,
        side_list,
        cluster_ids.reshape(row),
        damage.reshape(row),
        element_size.reshape(row),
        wave_speed.reshape(row),
        damage_rate.reshape(row),
    )
    final, new_damage, next_step = call(
        *(pltpu.with_memory_space_constraint(x, pltpu.HBM) for x in operands)
    )
    return final, new_damage.reshape(E), next_step.reshape(())


def solution(mesh):
    both = ("strike", "depth")
    in_specs = (
        P(None, None, both),
        P(None, None, None, both),
        P(None, None, None, None, both),
        P(),
        P(),
        P(),
        P(None, both),
        P(None, both),
        P(None, both),
        P(both),
        P(both),
        P(both),
        P(both),
        P(both),
    )
    out_specs = (P(None, None, both), P(both), P())
    body = functools.partial(shards, mesh.shape["strike"], mesh.shape["depth"])
    return jax.shard_map(body, mesh=mesh, in_specs=in_specs, out_specs=out_specs, check_vma=False)
```

```python
import functools

import jax
import jax.numpy as jnp
from jax import lax
from jax.experimental import pallas as pl
from jax.experimental.pallas import tpu as pltpu
from jax.sharding import PartitionSpec as P

COURANT = 1.0
Q = 9
B = 35
BP = 40
E = 128
HALF = 64
NSEL = 48
MESH = pl.DeviceIdType.MESH
f32, bf16 = jnp.float32, jnp.bfloat16
ROW_OF_SLOT = (1, 0, 3, 2)
START, HEIGHT = (0, 32), (32, 40)
SENT = 72
MARK = 38
CHUNKS = 1
PER = Q // CHUNKS
STAGES = ("strike", "depth", "depth", "strike")
LAST = ((0, 5),)
ROWS = (40, 24, 16, 8, 8)
SLOTS = (48, 32, 16, 16, 16)


def split(x):
    high = x.astype(bf16)
    return high, (x - high.astype(f32)).astype(bf16)


def third_of(slot):
    return 2 * slot if 3 * slot <= 128 else 128


def make_stack(matrix, slot):
    lane = lax.broadcasted_iota(jnp.int32, matrix.shape, 1)
    high, low = split(jnp.where(lane < slot, matrix, 0.0))
    high, low = high.astype(f32), low.astype(f32)
    if 3 * slot <= 128:
        return (high + pltpu.roll(high, slot, 1) + pltpu.roll(low, 2 * slot, 1)).astype(bf16)
    return jnp.concatenate([high + pltpu.roll(high, slot, 1), low], axis=1).astype(bf16)


def degree_of(index):
    degree = jnp.zeros_like(index)
    for first in (1, 4, 10, 20):
        degree = degree + jnp.where(index >= first, 1, 0)
    return degree


def kernel(
    n_strike,
    n_depth,
    dof_in,
    star_in,
    solver_in,
    stiff_in,
    local_in,
    flat_in,
    select_in,
    source_in,
    side_in,
    cluster_in,
    damage_in,
    size_in,
    speed_in,
    rate_in,
    dof_out,
    damage_out,
    step_out,
    dof_raw,
    star,
    solver,
    wide_stiff,
    wide_local,
    wide_flat,
    select,
    source,
    side,
    cluster,
    damage,
    size,
    speed,
    rate,
    mine,
    minima,
    side_got,
    dof,
    sent,
    sent_b,
    got,
    got_b,
    series_1,
    series_2,
    series_3,
    series_4,
    first,
    second,
    middle,
    stiff,
    flat,
    fine_weights,
    stack,
    matrix_0,
    matrix_1,
    matrix_2,
    matrix_u,
    applied,
    face_terms,
    part,
    chosen,
    pick,
    gathered_0,
    gathered_1,
    remote,
    load_sem,
    min_send,
    min_recv,
    side_send,
    side_recv,
    halo_send,
    halo_recv,
):
    s, d = lax.axis_index("strike"), lax.axis_index("depth")
    gathered = (gathered_0, gathered_1)
    series = (dof, series_1, series_2, series_3, series_4)

    loads = [
        pltpu.make_async_copy(src, dst, load_sem.at[index])
        for index, (src, dst) in enumerate(
            [
                (damage_in, damage),
                (size_in, size),
                (speed_in, speed),
                (dof_in, dof_raw),
                (side_in, side),
                (stiff_in, wide_stiff),
                (star_in, star),
                (cluster_in, cluster),
                (solver_in, solver),
                (local_in, wide_local),
                (flat_in, wide_flat),
                (select_in, select),
                (source_in, source),
                (rate_in, rate),
            ]
        )
    ]

    for load in loads[0:3]:
        load.start()

    barrier = pltpu.get_barrier_semaphore()
    groups = {"depth": (d, n_depth), "strike": (s, n_strike)}
    order = sorted(range(1, max(n_depth, n_strike)), key=lambda off: abs(off - n_depth / 2))
    for off in order:
        for axis, (me, count) in groups.items():
            if off < count:
                pl.semaphore_signal(
                    barrier, inc=1, device_id={axis: lax.rem(me + off, count)}, device_id_type=MESH
                )
    for load in loads[3:]:
        load.start()

    has = (s > 0, s < n_strike - 1, d > 0, d < n_depth - 1)
    towards = (
        (s < n_strike - 1, {"strike": lax.rem(s + 1, n_strike)}),
        (s > 0, {"strike": lax.rem(s + n_strike - 1, n_strike)}),
        (d < n_depth - 1, {"depth": lax.rem(d + 1, n_depth)}),
        (d > 0, {"depth": lax.rem(d + n_depth - 1, n_depth)}),
    )

    def min_copy(stage, off):
        axis = STAGES[stage]
        me, count = groups[axis]
        return pltpu.make_async_remote_copy(
            src_ref=mine.at[stage],
            dst_ref=minima.at[stage, off - 1],
            send_sem=min_send.at[stage, off],
            recv_sem=min_recv.at[stage],
            device_id={axis: lax.rem(me + off, count)},
            device_id_type=MESH,
        )

    def min_offsets(stage):
        return [off for off in order if off < groups[STAGES[stage]][1]]

    def min_start(stage, row):
        mine[stage] = row
        for off in min_offsets(stage):
            min_copy(stage, off).start()

    def min_finish(stage):
        axis = STAGES[stage]
        me, count = groups[axis]
        rows = [mine[stage]]
        if count > 1:
            others = minima.at[stage, pl.ds(0, count - 1)]
            pltpu.make_async_remote_copy(
                src_ref=others,
                dst_ref=others,
                send_sem=min_send.at[stage, 0],
                recv_sem=min_recv.at[stage],
                device_id={axis: lax.rem(me + 1, count)},
                device_id_type=MESH,
            ).wait_recv()
            rows += [minima[stage, other] for other in range(count - 1)]
        while len(rows) > 1:
            rows = [jnp.minimum(a, b) for a, b in zip(rows[::2], rows[1::2])] + rows[len(rows) // 2 * 2 :]
        return rows[0]

    def min_drain(stage):
        for off in min_offsets(stage):
            min_copy(stage, off).wait_send()

    def halo_copy(piece, chunk, k, where):
        if piece < 2:
            rows = pl.ds(chunk * PER, PER)
            height = pl.ds(START[piece], HEIGHT[piece])
            src, dst = sent.at[rows, height], got.at[k, rows, height]
        else:
            rows = pl.ds(LAST[chunk][0], LAST[chunk][1] - LAST[chunk][0])
            src, dst = sent_b.at[rows], got_b.at[k, rows]
        return pltpu.make_async_remote_copy(
            src_ref=src,
            dst_ref=dst,
            send_sem=halo_send.at[piece, chunk, k],
            recv_sem=halo_recv.at[piece, chunk, k],
            device_id=where,
            device_id_type=MESH,
        )

    def side_copy(k, where):
        return pltpu.make_async_remote_copy(
            src_ref=side,
            dst_ref=side_got.at[k],
            send_sem=side_send.at[k],
            recv_sem=side_recv.at[k],
            device_id=where,
            device_id_type=MESH,
        )

    def to_all(send, ks=range(4)):
        for k in ks:
            exists, where = towards[k]

            @pl.when(exists)
            def _(k=k, where=where):
                send(k, where)

    def from_all(receive):
        for k in range(4):

            @pl.when(has[k])
            def _(k=k):
                receive(k, towards[k][1])

    left_half = lax.broadcasted_iota(jnp.int32, (BP, E), 1) < HALF
    left_row = left_half[0:1]
    sub = lax.broadcasted_iota(jnp.int32, (BP, E), 0)
    lane = lax.broadcasted_iota(jnp.int32, (BP, E), 1)

    def swap(x):
        return pltpu.roll(x, HALF, 1)

    def twice(x):
        return jnp.where(left_half[0 : x.shape[0]], x, swap(x))

    for load in loads[0:3]:
        load.wait()
    gain = 1.0 - damage[...]
    own_ratio = size[...] / (speed[...] * jnp.sqrt(gain))
    pl.semaphore_wait(barrier, n_depth + n_strike - 2)
    min_start(0, own_ratio)
    loads[3].wait()
    for q in range(Q):
        sent[q, 0:32, :] = dof_raw[q, 0:32, :]
    for ks in ((0, 1), (2, 3)):
        for chunk in range(CHUNKS):
            to_all(lambda k, where: halo_copy(0, chunk, k, where).start(), ks)
    loads[4].wait()
    to_all(lambda k, where: side_copy(k, where).start())

    for k in range(4):

        @pl.when(jnp.logical_not(has[k]))
        def _(k=k):
            got[k] = jnp.zeros((Q, SENT, E), f32)
            got_b[k] = jnp.zeros((5, BP, E), f32)
            side_got[k] = jnp.full((4, E), -1, jnp.int32)

    stack[96:128, :] = jnp.zeros((32, Q * E), bf16)
    stack[176:256, :] = jnp.zeros((80, Q * E), bf16)
    stiff[...] = jnp.zeros((7, E, E), f32)

    loads[7].wait()
    coarse = jnp.where(cluster[...] != 0, 1.0, 0.0)
    for q in range(Q):
        dof[q, 32:BP, :] = jnp.zeros((8, E), f32)
        dof[q, 0:B, :] = dof_raw[q]

    loads[5].wait()
    inside = jnp.logical_and(sub < B, lane < B)
    keep = jnp.logical_and(inside, degree_of(sub) < degree_of(lane))
    for c in range(3):
        stiff[c, 0:B, 0:B] = wide_stiff[c]
        kept = jnp.where(keep, stiff[c, 0:BP, :], 0.0)
        stiff[c, 0:BP, :] = kept
        matrix_0[c * 24 : (c + 1) * 24, :] = kept[0:24]
        matrix_1[c * 16 : (c + 1) * 16, :] = jnp.where(lane[0:16] < 20, kept[0:16], 0.0)
        matrix_2[c * 8 : (c + 1) * 8, :] = jnp.where(lane[0:8] < 10, kept[0:8], 0.0)

    def put_stack(source_rows, slot):
        third = third_of(slot)
        for p in range(Q):
            x = source_rows(p)
            if x.shape[0] < slot:
                x = jnp.concatenate([x, jnp.zeros((slot - x.shape[0], E), f32)], axis=0)
            high, low = split(x)
            columns = pl.ds(p * E, E)
            stack[0:slot, columns] = high
            stack[slot : 2 * slot, columns] = low
            stack[third : third + slot, columns] = high

    def stacked_dot(left, slot):
        rows = 256 if 3 * slot > 128 else 3 * slot
        return jnp.dot(left[:, 0:rows], stack[0:rows, :], preferred_element_type=f32)

    def contract(weight, pieces, rows, sums):
        def body(p, sums):
            sums = list(sums)
            for g in pieces:
                field = applied[g, p, 0:rows, :]
                for q in range(Q):
                    sums[q] = sums[q] + weight(q, p, g) * field
            return tuple(sums)

        if rows <= 24:
            for p in range(Q):
                sums = body(p, sums)
            return sums
        return lax.fori_loop(0, Q, body, tuple(sums))

    def nothing(rows):
        return [jnp.zeros((rows, E), f32) for _ in range(Q)]

    def scaled(q, x, by):
        return x * by if q < 6 else x

    def star_weight(q, p, c):
        return star[q, p, c : c + 1, :]

    pack_rows = (16, 18, 0, 2, 4, 6, 12, 14)

    def fine_weight(shift):
        def weight(q, p, g):
            row = pack_rows[g + shift]
            return fine_weights[q, p, row : row + 1, :]

        return weight

    def derive(source_rows, order_in, target, fine):
        matrix = (matrix_0, matrix_1, matrix_2, matrix_2)[order_in]
        rows, slot = (24, 16, 8, 8)[order_in], SLOTS[order_in]
        put_stack(source_rows, slot)
        product = stacked_dot(make_stack(matrix[...], slot), slot)
        for p in range(Q):
            pieces = [product[c * rows : (c + 1) * rows, p * E : (p + 1) * E] for c in range(3)]
            if fine:
                pieces = [jnp.where(left_half[0:rows], pieces[0], pieces[1]), pieces[2]]
            for g, piece in enumerate(pieces):
                applied[g, p, 0:rows, :] = piece
        if fine:
            sums = contract(fine_weight(0), range(2), rows, nothing(rows))
        else:
            sums = contract(star_weight, range(3), rows, nothing(rows))
        for q in range(Q):
            total = sums[q] + swap(sums[q]) if fine else sums[q]
            target[q] = -scaled(q, total, gain_fine if fine else gain)

    loads[6].wait()
    for index in range(4):
        derive(lambda p, index=index: series[index][p], index, series[index + 1], False)
    sub8 = lax.broadcasted_iota(jnp.int32, (8, E), 0)
    for q in range(Q):
        turned = pltpu.roll(series_2[q, 0:8], 4, 0)
        sent[q, 32:40, :] = (
            dof[q, 32:BP, :] + pltpu.roll(series_3[q], 3, 0) + pltpu.roll(series_4[q], 7, 0)
        )
        sent[q, 40:56, :] = series_1[q, 0:16]
        sent[q, 56:64, :] = series_1[q, 16:24] + jnp.where(sub8 >= 4, turned, 0.0)
        sent[q, 64:72, :] = jnp.where(sub8 < 4, turned, 0.0) + pltpu.roll(series_2[q, 8:16], 4, 0)
    sent[0, 32 + MARK : 33 + MARK, :] = coarse
    for chunk in range(CHUNKS):
        to_all(lambda k, where: halo_copy(1, chunk, k, where).start(), (0, 1))

    loads[8].wait()

    left8 = left_half[0:8]
    row8 = lax.broadcasted_iota(jnp.int32, (8, E), 0)

    def pack(q, carry):
        for p in range(Q):
            both = jnp.concatenate([solver[0, q, p], solver[1, q, p]], axis=0)
            turned = swap(both)
            fine_weights[q, p, 0:8, :] = jnp.where(left8, both, pltpu.roll(turned, 7, 0))
            fine_weights[q, p, 8:16, :] = jnp.where(left8, turned, pltpu.roll(both, 7, 0))
            ways = jnp.concatenate([star[q, p], jnp.zeros((5, E), f32)], axis=0)
            other = jnp.where(row8 == 0, pltpu.roll(swap(ways), 7, 0), 0.0)
            fine_weights[q, p, 16:24, :] = jnp.where(left8, ways, other)
        return carry

    lax.fori_loop(0, Q, pack, 0)
    gain_fine = twice(gain)

    loads[9].wait()
    for c in range(3):
        matrix_u[c * BP : (c + 1) * BP, :] = jnp.transpose(stiff[c])[0:BP]
    for f in range(4):
        stiff[3 + f, 0:B, 0:B] = wide_local[:, f, :]
        matrix_u[(3 + f) * BP : (4 + f) * BP, :] = -stiff[3 + f, 0:BP, :]

    def own_fine():
        put_stack(lambda p: twice(first[p]), 48)
        product = stacked_dot(make_stack(matrix_u[...], 48), 48)
        for p in range(Q):
            pieces = [product[g * BP : (g + 1) * BP, p * E : (p + 1) * E] for g in range(7)]
            applied[0, p] = jnp.where(left_half, pieces[0], pieces[1])
            applied[1, p] = pieces[2]
            applied[2, p] = jnp.where(left_half, pieces[3], pieces[4])
            applied[3, p] = jnp.where(left_half, pieces[5], pieces[6])

    def paired(ref):
        rows = [ref[f : f + 1, :] for f in range(4)]
        return [
            jnp.where(left_row, rows[0], swap(rows[1])),
            jnp.where(left_row, rows[2], swap(rows[3])),
            jnp.where(left_row, swap(rows[0]), rows[1]),
            jnp.where(left_row, swap(rows[2]), rows[3]),
        ]

    loads[12].wait()
    place = lax.broadcasted_iota(jnp.int32, (E, E), 0)

    def one_hot(mask):
        return jnp.where(mask, 1.0, 0.0).astype(bf16)

    sources = paired(source)

    def point():
        for k in range(4):
            right = jnp.concatenate([one_hot(place == row - (E + k * E)) for row in sources], axis=1)
            row = ROW_OF_SLOT[k]
            left = one_hot(place == side_got[k, row : row + 1, :])
            right = jnp.dot(left, right, preferred_element_type=f32).astype(bf16)
            pick[k, 0:E, :] = right
            pick[k, E : 2 * E, :] = right

    from_all(lambda k, where: side_copy(k, where).wait_recv())
    point()
    row = min_finish(0)
    min_start(1, row)
    for chunk in range(CHUNKS):
        to_all(lambda k, where: halo_copy(1, chunk, k, where).start(), (2, 3))

    loads[11].wait()
    selects = paired(select)
    loads[10].wait()
    flat[...] = jnp.zeros((B * BP, E), f32)
    for i in range(B):
        flat[pl.ds(i, B, stride=BP), 0:NSEL] = wide_flat[i]
    number = lax.rem(lax.broadcasted_iota(jnp.int32, (E, E), 0), NSEL)
    usable = lax.broadcasted_iota(jnp.int32, (E, E), 0) < 2 * NSEL
    hot = jnp.concatenate(
        [
            jnp.where(jnp.logical_and(number == row, usable), -1.0, 0.0).astype(bf16)
            for row in selects
        ],
        axis=1,
    )

    def choose(index, carry):
        rows = pl.ds(pl.multiple_of(index * 200, 8), 200)
        high, low = split(flat[rows, :])
        left = (high.astype(f32) + pltpu.roll(low.astype(f32), NSEL, 1)).astype(bf16)
        product = jnp.dot(left, hot, preferred_element_type=f32)
        for g in range(4):
            chosen[g, rows, :] = product[:, g * E : (g + 1) * E]
        return carry

    lax.fori_loop(0, 7, choose, 0)

    def gather(blocks):
        total = None
        for k in range(4):
            high, low = split(blocks[k])
            left = jnp.concatenate([high, low], axis=1)
            value = jnp.dot(left, pick[k], preferred_element_type=f32)
            total = value if total is None else total + value
        return total

    def gather_series(piece):
        height = HEIGHT[piece]
        for part_of in range(3):
            rows = slice(part_of * 3, part_of * 3 + 3)
            total = gather(
                [got[k, rows, START[piece] : START[piece] + height].reshape(3 * height, E) for k in range(4)]
            )
            for g in range(4):
                where = slice(part_of * 3 * height, (part_of + 1) * 3 * height)
                gathered[piece][g, where, :] = total[:, g * E : (g + 1) * E]

    def near(source_row, first_j, count, g, ps, sums):
        for j in range(count):
            matrix = chosen[g, (first_j + j) * BP : (first_j + j + 1) * BP, :]
            for n, p in enumerate(ps):
                sums[n] = sums[n] + matrix * source_row(p, j)
        return sums

    for chunk in range(CHUNKS):
        from_all(lambda k, where: halo_copy(0, chunk, k, where).wait_recv())

    gather_series(0)

    def face_before(g, carry):
        sums = [jnp.zeros((BP, E), f32) for _ in range(Q)]
        sums = near(lambda p, j: gathered_0[g, p * 32 + j : p * 32 + j + 1, :], 0, 32, g, range(Q), sums)
        for p in range(Q):
            face_terms[g, p] = sums[p]
        return carry

    lax.fori_loop(0, 2, face_before, 0)

    step = jnp.min(min_finish(1), axis=1, keepdims=True) * COURANT
    step = jnp.broadcast_to(step, (1, E))
    powers, value = [], 1.0
    for power in range(5):
        value = value * step / (power + 1)
        powers.append(value)
    late = [powers[k] * (2.0 ** (k + 1) - 1.0) for k in range(5)]

    def taylor(base, q, weight):
        whole = weight[0] * base[q]
        low = whole[0:8] + weight[1] * series_1[q, 0:8] + weight[2] * series_2[q, 0:8]
        low = low + weight[3] * series_3[q] + weight[4] * series_4[q]
        mid = whole[8:16] + weight[1] * series_1[q, 8:16] + weight[2] * series_2[q, 8:16]
        top = whole[16:24] + weight[1] * series_1[q, 16:24]
        return jnp.concatenate([low, mid, top, whole[24:BP]], axis=0)

    fine = coarse < 0.5
    for q in range(Q):
        first[q] = taylor(dof, q, powers)
        second[q] = taylor(dof, q, late)
    own_fine()
    changes = contract(fine_weight(0), range(4), BP, nothing(BP))
    for q in range(Q):
        part[0, q] = changes[q]

    def series_tiles(g, p):
        mixed = gathered_1[g, p * 40 : p * 40 + 8, :]
        high = [gathered_1[g, p * 40 + 8 * t : p * 40 + 8 * t + 8, :] for t in range(1, 5)]
        turned = pltpu.roll(high[3], 4, 0)
        d_1 = (high[0], high[1], jnp.where(sub8 < 4, high[2], 0.0))
        d_2 = (
            jnp.where(sub8 < 4, pltpu.roll(high[2], 4, 0), turned),
            jnp.where(sub8 < 2, turned, 0.0),
        )
        d_3 = jnp.where(sub8 < 4, pltpu.roll(mixed, 5, 0), 0.0)
        d_4 = jnp.where(sub8 < 1, pltpu.roll(mixed, 1, 0), 0.0)
        return mixed, d_1, d_2, d_3, d_4

    def summed_tiles(tiles, weight):
        mixed, d_1, d_2, d_3, d_4 = tiles
        return (
            weight[1] * d_1[0] + weight[2] * d_2[0] + weight[3] * d_3 + weight[4] * d_4,
            weight[1] * d_1[1] + weight[2] * d_2[1],
            weight[1] * d_1[2],
            weight[0] * mixed,
        )

    for chunk in range(CHUNKS):
        ps = range(chunk * PER, (chunk + 1) * PER)
        from_all(lambda k, where: halo_copy(1, chunk, k, where).wait_recv())
        gather_series(1)
        for g in range(2):
            for p in ps:
                for t, tile in enumerate(summed_tiles(series_tiles(g, p), powers)):
                    remote[g, p * BP + 8 * t : p * BP + 8 * t + 8, :] = tile

        def face_after(g, carry, ps=ps):
            sums = [powers[0] * face_terms[g, p] for p in ps]
            sums = near(lambda p, j: remote[g, p * BP + j : p * BP + j + 1, :], 0, 20, g, ps, sums)
            sums = near(lambda p, j: remote[g, p * BP + 24 + j : p * BP + 25 + j, :], 32, 3, g, ps, sums)
            for n, p in enumerate(ps):
                applied[4 + g, p] = sums[n]
            return carry

        lax.fori_loop(0, 2, face_after, 0)
    changes = contract(fine_weight(0), range(4, 6), BP, [part[0, q] for q in range(Q)])
    for q in range(Q):
        change = changes[q] + swap(changes[q])
        middle[q] = twice(dof[q]) + scaled(q, change, gain_fine)
    for index in range(4):
        base = middle if index == 0 else series[index]
        derive(lambda p, base=base: base[p], index, series[index + 1], True)
    fine_left = jnp.logical_and(fine, left_row)
    for q in range(Q):
        applied[10, q] = taylor(middle, q, powers)
        second[q] = jnp.where(fine_left, applied[10, q], second[q])

    energy = jnp.zeros((1, E), f32)
    for q in range(6):
        mean = (first[q, 0:1, :] + second[q, 0:1, :]) / (2.0 * step)
        energy = energy + mean * mean
    loads[13].wait()
    exposure = 2.0 * step * rate[...] * energy / (1.0 + energy)
    new_gain = gain * jnp.exp(-exposure)
    min_start(2, size[...] / (speed[...] * jnp.sqrt(new_gain)))
    damage_out[...] = 1.0 - new_gain

    fine_both = twice(jnp.where(fine, 1.0, 0.0))
    for n in range(5):
        other = applied[10, 2 * n + 1] if n < 4 else jnp.zeros((BP, E), f32)
        sent_b[n] = jnp.where(left_half, applied[10, 2 * n], other) * fine_both
    for chunk in range(CHUNKS):
        to_all(lambda k, where: halo_copy(2, chunk, k, where).start())

    put_stack(lambda p: second[p] + coarse * first[p], 48)
    product = stacked_dot(make_stack(matrix_u[...], 48), 48)
    for g in range(7):
        for p in range(Q):
            applied[g, p] = product[g * BP : (g + 1) * BP, p * E : (p + 1) * E]

    def own_weight(q, p, g):
        return star[q, p, g : g + 1, :] if g < 3 else solver[0, q, p, g - 3 : g - 2, :]

    sums = contract(own_weight, range(7), BP, nothing(BP))
    for q in range(Q):
        part[0, q] = sums[q]
    for q in range(Q):
        base = jnp.where(fine_left, middle[q], dof[q])
        middle[q] = base


    coarse_halves = [
        jnp.where(left_row, coarse, swap(coarse)),
        jnp.where(left_row, swap(coarse), coarse),
    ]
    for g in range(4):
        theirs = gathered_1[g, MARK : MARK + 1, :]
        weight = [late[k] * theirs + powers[k] * coarse_halves[g // 2] for k in range(5)]
        for p in range(Q):
            tiles = summed_tiles(series_tiles(g, p), weight)
            value = [weight[0] * gathered_0[g, p * 32 + 8 * t : p * 32 + 8 * t + 8, :] for t in range(4)]
            value = [value[0] + tiles[0], value[1] + tiles[1], value[2] + tiles[2], value[3], tiles[3]]
            for t in range(5):
                remote[g, p * BP + 8 * t : p * BP + 8 * t + 8, :] = value[t]

    for k in range(4):
        pick[k, HALF:E, :] = jnp.zeros((HALF, 4 * E), bf16)
        pick[k, E + HALF : 2 * E, :] = jnp.zeros((HALF, 4 * E), bf16)

    for stage in range(2):
        min_drain(stage)
    to_all(lambda k, where: side_copy(k, where).wait_send())
    for piece in range(2):
        for chunk in range(CHUNKS):
            to_all(lambda k, where: halo_copy(piece, chunk, k, where).wait_send())

    row = min_finish(2)
    min_start(3, row)
    for chunk, (start, stop) in enumerate(LAST):
        from_all(lambda k, where: halo_copy(2, chunk, k, where).wait_recv())
        ps = range(2 * start, min(2 * stop, Q))
        for n in range(start, stop):
            blocks = [got_b[k, n] for k in range(4)]
            total = gather([jnp.concatenate([x, swap(x)], axis=0) for x in blocks])
            for half in range(2 if n < 4 else 1):
                rows = slice((2 * n + half) * BP, (2 * n + half + 1) * BP)
                for g in range(4):
                    value = total[half * BP : (half + 1) * BP, g * E : (g + 1) * E]
                    remote[g, rows, :] = remote[g, rows, :] + value

        def last_face(g, carry, ps=ps):
            sums = [jnp.zeros((BP, E), f32) for _ in ps]
            sums = near(lambda p, j: remote[g, p * BP + j : p * BP + j + 1, :], 0, B, g, ps, sums)
            for n, p in enumerate(ps):
                applied[g, p] = sums[n]
            return carry

        lax.fori_loop(0, 4, last_face, 0)
    left_sums = contract(fine_weight(4), range(2), BP, nothing(BP))
    for q in range(Q):
        total = left_sums[q]
        part[1, q] = total + swap(total)
    right_sums = contract(fine_weight(4), range(2, 4), BP, nothing(BP))
    for q in range(Q):
        total = right_sums[q]
        value = part[0, q] + jnp.where(left_half, part[1, q], total + swap(total))
        dof_out[q] = (middle[q] + scaled(q, value, gain))[0:B]

    min_drain(2)
    for chunk in range(CHUNKS):
        to_all(lambda k, where: halo_copy(2, chunk, k, where).wait_send())
    step_out[...] = COURANT * jnp.min(min_finish(3), axis=1, keepdims=True)
    min_drain(3)


def shards(
    n_strike,
    n_depth,
    dof_values,
    star_matrices,
    flux_solvers,
    stiffness,
    flux_local,
    flux_neighbour,
    flux_select,
    face_source,
    side_list,
    cluster_ids,
    damage,
    element_size,
    wave_speed,
    damage_rate,
):
    out_shape = (
        jax.ShapeDtypeStruct((Q, B, E), f32),
        jax.ShapeDtypeStruct((1, E), f32),
        jax.ShapeDtypeStruct((1, 1), f32),
    )
    most = max(n_strike, n_depth)
    vmem = pltpu.VMEM
    dma = pltpu.SemaphoreType.DMA
    call = pl.pallas_call(
        functools.partial(kernel, n_strike, n_depth),
        out_shape=out_shape,
        in_specs=[pl.BlockSpec(memory_space=pltpu.HBM)] * 14,
        out_specs=tuple(pl.BlockSpec(memory_space=pltpu.VMEM) for _ in range(3)),
        scratch_shapes=[
            vmem((Q, B, E), f32),
            vmem((Q, Q, 3, E), f32),
            vmem((2, Q, Q, 4, E), f32),
            vmem((3, B, B), f32),
            vmem((B, 4, B), f32),
            vmem((B, B, NSEL), f32),
            vmem((4, E), jnp.int32),
            vmem((4, E), jnp.int32),
            vmem((4, E), jnp.int32),
            vmem((1, E), jnp.int32),
            vmem((1, E), f32),
            vmem((1, E), f32),
            vmem((1, E), f32),
            vmem((1, E), f32),
            vmem((4, 1, E), f32),
            vmem((4, most - 1 if most > 1 else 1, 1, E), f32),
            vmem((4, 4, E), jnp.int32),
            vmem((Q, BP, E), f32),
            vmem((Q, SENT, E), f32),
            vmem((5, BP, E), f32),
            vmem((4, Q, SENT, E), f32),
            vmem((4, 5, BP, E), f32),
            vmem((Q, 24, E), f32),
            vmem((Q, 16, E), f32),
            vmem((Q, 8, E), f32),
            vmem((Q, 8, E), f32),
            vmem((Q, BP, E), f32),
            vmem((Q, BP, E), f32),
            vmem((Q, BP, E), f32),
            vmem((7, E, E), f32),
            vmem((B * BP, E), f32),
            vmem((Q, Q, 24, E), f32),
            vmem((256, Q * E), bf16),
            vmem((72, E), f32),
            vmem((48, E), f32),
            vmem((24, E), f32),
            vmem((280, E), f32),
            vmem((11, Q, BP, E), f32),
            vmem((2, Q, BP, E), f32),
            vmem((2, Q, BP, E), f32),
            vmem((4, B * BP, E), f32),
            vmem((4, 2 * E, 4 * E), bf16),
            vmem((4, Q * HEIGHT[0], E), f32),
            vmem((4, Q * HEIGHT[1], E), f32),
            vmem((4, Q * BP, E), f32),
            dma((14,)),
            dma((4, most)),
            dma((4,)),
            dma((4,)),
            dma((4,)),
            dma((3, CHUNKS, 4)),
            dma((3, CHUNKS, 4)),
        ],
        compiler_params=pltpu.CompilerParams(
            collective_id=0, has_side_effects=True, vmem_limit_bytes=32 * 1024 * 1024
        ),
    )
    row = (1, E)
    operands = (
        dof_values,
        jnp.transpose(star_matrices, (1, 2, 0, 3)),
        jnp.transpose(flux_solvers, (0, 2, 3, 1, 4)),
        stiffness,
        jnp.transpose(flux_local, (1, 0, 2)),
        jnp.transpose(flux_neighbour, (1, 2, 0)),
        flux_select,
        face_source,
        side_list,
        cluster_ids.reshape(row),
        damage.reshape(row),
        element_size.reshape(row),
        wave_speed.reshape(row),
        damage_rate.reshape(row),
    )
    final, new_damage, next_step = call(
        *(pltpu.with_memory_space_constraint(x, pltpu.HBM) for x in operands)
    )
    return final, new_damage.reshape(E), next_step.reshape(())


def solution(mesh):
    both = ("strike", "depth")
    in_specs = (
        P(None, None, both),
        P(None, None, None, both),
        P(None, None, None, None, both),
        P(),
        P(),
        P(),
        P(None, both),
        P(None, both),
        P(None, both),
        P(both),
        P(both),
        P(both),
        P(both),
        P(both),
    )
    out_specs = (P(None, None, both), P(both), P())
    body = functools.partial(shards, mesh.shape["strike"], mesh.shape["depth"])
    return jax.shard_map(body, mesh=mesh, in_specs=in_specs, out_specs=out_specs, check_vma=False)
```
